256 devices in a mesh: ctx: 32 (over y, z), ch: 8 (over x, core).
Axes of the slice: x: 4, y: 4, z: 8, core: 2. Of those that a mesh axis runs over, the one named last changes fastest.
Arguments:
- query_in: bfloat16 [4096, 8192], P('ch', 'ctx'), may hold values from -6 to 6
- key_in: bfloat16 [4096, 8192], P('ch', 'ctx'), may hold values from -6 to 6
- value_in: bfloat16 [4096, 8192], P('ch', 'ctx'), may hold values from -6 to 6
- short_taps: float32 [3, 4096, 3], P(None, 'ch'), may hold values from -3 to 3
- modal_residue: float32 [4096, 16], P('ch'), may hold values from -2.5 to 2.5
- mode_damping_speed: float32 [4096, 16], P('ch'), may hold values from 6.1035156e-05 to 0.05
- skip_gain: float32 [4096], P('ch'), may hold values from 0.5 to 1.5
- out_weight: bfloat16 [4096, 4096], P('ch'), may hold values from -0.125 to 0.125
Outputs:
- mixed: bfloat16 [4096, 8192], P('ch', 'ctx')
The draws below stay inside these ranges and needn't reach their ends.
All inputs are finite; a program needn't handle non-finite values.
Results may differ from the reference program's by a relative error of at most 0.01.
Values may be sent and summed in bfloat16 or wider, within the bound.
No kernel may reach another device: no remote copies, remote signals or barrier semaphores. Data moves between devices by JAX's collectives and lax.ppermute only.
A program may use at most 128 MiB of HBM per device.

```python
import math
import jax
import jax.numpy as jnp

ORDER = 16
SEQUENCE_SPAN = 8192
CHANNELS = 4096


def raised(result, key, source, target, shards_of, factor):
    def block_of(dim):
        return (jnp.arange(result.shape[dim]) // (result.shape[dim] // shards_of)).reshape((-1,) + (1,) * (result.ndim - 1 - dim))

    one_side = jax.random.permutation(key, shards_of)[block_of(target)]
    far = (block_of(target) + shards_of // 2) % shards_of
    return jnp.where((block_of(source) == one_side) | (block_of(source) == far), factor * result, result)


def block_levels(rng, extent, cuts, low, top_value):
    factor_of, own = 1.0, jax.random.fold_in(rng, 6)
    for position, shards_of in cuts:
        heights = jnp.exp(jax.random.uniform(jax.random.fold_in(own, position), (shards_of,), jnp.float32, low / len(cuts), top_value / len(cuts)))
        factor_of = factor_of * jnp.repeat(heights, extent[position] // shards_of).reshape([-1 if axis == position else 1 for axis in range(len(extent))])
    return factor_of


def normal_values(own_key, extent, spread, limit, cuts=(), held_as=jnp.bfloat16):
    values = spread * jax.random.normal(own_key, extent, jnp.float32)
    if cuts:
        values = values * block_levels(own_key, extent, cuts, -0.22, 0.18)
    return jnp.clip(values, -limit, limit).astype(held_as)


def noise_with(stream_key, shape, scale, bound, shards, heavy, dtype=jnp.bfloat16):
    entries = scale * jax.random.normal(stream_key, shape, jnp.float32)
    if shards:
        entries = entries * block_levels(stream_key, shape, shards, -0.22, 0.18)
    return jnp.clip(raised(entries, jax.random.fold_in(stream_key, 3), *heavy), -bound, bound).astype(dtype)


def setup_inputs(seed: int = 0) -> dict:
    key_of = jax.random.split(jax.random.key(seed), 9)
    return {
        "query_in": normal_values(key_of[0], (CHANNELS, SEQUENCE_SPAN), 1.0, 6.0, ((0, 8), (1, 32))),
        "key_in": normal_values(key_of[1], (CHANNELS, SEQUENCE_SPAN), 1.0, 6.0, ((0, 8), (1, 32))),
        "value_in": normal_values(key_of[2], (CHANNELS, SEQUENCE_SPAN), 1.0, 6.0, ((0, 8), (1, 32))),
        "short_taps": normal_values(key_of[3], (3, CHANNELS, 3), 0.6, 3.0, ((1, 8),), jnp.float32),
        "modal_residue": normal_values(key_of[4], (CHANNELS, ORDER), 0.35, 2.5, ((0, 8),), jnp.float32),
        "mode_damping_speed": jnp.clip(jnp.exp(math.log(0.05) - 6.7083283 * jax.random.uniform(key_of[5], (CHANNELS, ORDER), jnp.float32) ** block_levels(key_of[5], (CHANNELS, ORDER), ((0, 8),), -0.2, 0.2)), 6.103515625e-05, 0.05),
        "skip_gain": jnp.clip(0.5 + 1.0 * jax.random.uniform(key_of[6], (CHANNELS,), jnp.float32) ** block_levels(key_of[6], (CHANNELS,), ((0, 8),), -0.2, 0.2), 0.5, 1.5),
        "out_weight": noise_with(key_of[7], (CHANNELS, CHANNELS), CHANNELS ** -0.5, 0.125, ((0, 8),), (0, 1, 8, 2.0)),
    }


def reference(query_in, key_in, value_in, short_taps, modal_residue, mode_damping_speed, skip_gain, out_weight):
    streams = jnp.stack([query_in, key_in, value_in]).astype(jnp.float32)
    padded = jnp.pad(streams, ((0, 0), (0, 0), (2, 0)))
    filtered = short_taps[:, :, 0:1] * padded[:, :, 2:] + short_taps[:, :, 1:2] * padded[:, :, 1:-1] + short_taps[:, :, 2:3] * padded[:, :, :-2]
    gated_input = filtered[1] * filtered[2]
    sample_moments = jnp.arange(SEQUENCE_SPAN).astype(jnp.float32)
    response_coefficients = modal_residue * jnp.sqrt(mode_damping_speed)
    extended_response = jnp.zeros((CHANNELS, SEQUENCE_SPAN), jnp.float32)
    for mode_count in range(ORDER):
        damping_vertical_vector = mode_damping_speed[:, mode_count:mode_count + 1]
        extended_response = extended_response + response_coefficients[:, mode_count:mode_count + 1] * jnp.exp(-damping_vertical_vector * sample_moments[None, :])
    spectrum = jnp.fft.rfft(gated_input, n=2 * SEQUENCE_SPAN, axis=1) * jnp.fft.rfft(extended_response, n=2 * SEQUENCE_SPAN, axis=1)
    convolved = jnp.fft.irfft(spectrum, n=2 * SEQUENCE_SPAN, axis=1)[:, :SEQUENCE_SPAN]
    mixed_in = (filtered[0] * (convolved + skip_gain[:, None] * gated_input)).astype(jnp.bfloat16)
    return jnp.dot(out_weight.T, mixed_in, preferred_element_type=jnp.float32).astype(jnp.bfloat16)
```

```python
import functools

import jax
import jax.numpy as jnp
from jax import lax
from jax.experimental import pallas as pl
from jax.experimental.pallas import tpu as pltpu
from jax.sharding import PartitionSpec as P

SEGMENTS = 8
LANES = 128
ORDER = 16
ROW = 8
SCOPED = 16 * 2**20
F32 = jnp.float32
BF16 = jnp.bfloat16
NT = (((1,), (1,)), ((), ()))
TN = (((0,), (0,)), ((), ()))

STEPS = ((1, 1), (2, 2), (4, 7))
DECAY, FADE, WEIGHT, GROWTH, OVER_Z, OVER_Y = 0, 1, 4, 5, 7, 22
TABLES = 28
SKIP, GROWN, FIRST = 9, 10, 11
EDGES = 32


def call(kernel, name, out, scratch=(), held=True, outside=(), unread=()):
    whole = pl.BlockSpec(memory_space=pltpu.VMEM)
    place = (lambda o: pltpu.VMEM(o.shape, o.dtype)) if held else (lambda o: o)

    def run(*args):
        spaces = [
            pl.ANY if i in unread else pltpu.HBM if i in outside else pltpu.VMEM
            for i in range(len(args))
        ]
        return pl.pallas_call(
            kernel,
            in_specs=[pl.BlockSpec(memory_space=space) for space in spaces],
            out_specs=jax.tree.map(lambda _: whole, out),
            out_shape=jax.tree.map(place, out),
            scratch_shapes=list(scratch),
            compiler_params=pltpu.CompilerParams(vmem_limit_bytes=SCOPED),
            name=name,
        )(*(pltpu.with_memory_space_constraint(a, space) for a, space in zip(args, spaces)))

    return run


def order_matrix(span):
    steps = span // SEGMENTS
    row = lax.broadcasted_iota(jnp.int32, (span, span), 0)
    col = lax.broadcasted_iota(jnp.int32, (span, span), 1)
    return jnp.where(col == (row & (SEGMENTS - 1)) * steps + (row >> 3), 1.0, 0.0).astype(BF16)


def segment_index():
    return lax.broadcasted_iota(jnp.int32, (SEGMENTS, LANES), 0)


def by_group(channels, body):
    def step(g, nothing):
        body(pl.ds(pl.multiple_of(g * LANES, LANES), LANES))
        return nothing

    lax.fori_loop(0, channels // LANES, step, 0)


def place_of():
    here = lax.axis_index("ctx")
    return here // ROW, lax.rem(here, ROW)


def fill_tables(damping, residue, span, tables):
    y, z = place_of()

    def fade(by):
        return jnp.exp(-damping * by)

    def only(flag, value):
        return jnp.where(flag, value, 0.0)

    tables[DECAY] = fade(1.0)
    for i in range(3):
        tables[FADE + i] = fade(float((span // SEGMENTS) << i))
    tables[WEIGHT] = residue * jnp.sqrt(damping)
    tables[GROWTH] = fade(-1.0)
    tables[GROWTH + 1] = fade(-2.0)
    for j, (size, _) in enumerate(STEPS):
        at = OVER_Z + 5 * j
        older = (z & size) != 0
        ahead = (z & (size - 1)) * span
        whole = fade(float(size * span))
        tables[at] = only(older, fade(ahead.astype(F32)))
        seen = jnp.maximum(ahead - 2, 0).astype(F32)
        tables[at + 1] = only(older & (ahead > 0), fade(seen))
        tables[at + 2] = jnp.where(older, whole, 1.0)
        tables[at + 3] = jnp.where(older, 1.0, whole)
        tables[at + 4] = fade(float(size * span - 2))
    for s in range(3):
        ahead = (ROW * s + z) * span
        tables[OVER_Y + s] = only(y >= s + 1, fade(ahead.astype(F32)))
        seen = jnp.maximum(ahead - 2, 0).astype(F32)
        tables[OVER_Y + 3 + s] = only((y >= s + 1) & (ahead > 0), fade(seen))


def states_kernel(
    key_hbm,
    value_hbm,
    query_hbm,
    taps_hbm,
    damping_hbm,
    residue_hbm,
    skip_hbm,
    message,
    gated,
    params,
    tables,
    raw,
    tail,
    taps_in,
    damping,
    residue,
    skip,
    streams,
    state,
    edges,
    sems,
):
    channels, span = key_hbm.shape
    steps = span // SEGMENTS
    copies = [
        pltpu.make_async_copy(src, dst, sems.at[i])
        for i, (src, dst) in enumerate(
            (
                (damping_hbm, damping),
                (residue_hbm, residue),
                (key_hbm, raw.at[0]),
                (value_hbm, raw.at[1]),
                (taps_hbm, taps_in),
                (skip_hbm, skip),
                (query_hbm.at[:, span - LANES :], tail),
            )
        )
    ]
    for c in copies:
        c.start()
    order = order_matrix(span)
    for c in copies[:2]:
        c.wait()
    fill_tables(damping[...], residue[...], span, tables)
    for c in copies[2:]:
        c.wait()
    for s in range(2):
        streams[s] = lax.dot_general(order, raw[s], NT, preferred_element_type=F32)
    segment = segment_index()
    params[...] = jnp.zeros_like(params)
    for i in range(9):
        params[i : i + 1, :] = taps_in[(1 + i // 3) % 3, i % 3, :][None, :]
    params[SKIP : SKIP + 1, :] = skip[...]
    params[GROWN : GROWN + 1, :] = jnp.sum(
        tables[WEIGHT] * tables[GROWTH], axis=0, keepdims=True
    )

    def group(lanes):
        taps = [params[i : i + 1, lanes] for i in range(6)]
        decay = [tables[DECAY, r : r + 1, lanes] for r in range(ORDER)]

        def at(s, a):
            if a >= 0:
                return streams[s, a * SEGMENTS : (a + 1) * SEGMENTS, lanes]
            rolled = pltpu.roll(at(s, a + steps), 1, 0)
            return jnp.where(segment == 0, 0.0, rolled)

        held = [jnp.zeros((SEGMENTS, LANES), F32) for _ in range(ORDER)]
        for a in range(steps):
            f = [
                taps[3 * s] * at(s, a)
                + taps[3 * s + 1] * at(s, a - 1)
                + taps[3 * s + 2] * at(s, a - 2)
                for s in range(2)
            ]
            u = f[0] * f[1]
            if a < 2:
                params[FIRST + a : FIRST + a + 1, lanes] = f[0][0:1]
                params[FIRST + 2 + a : FIRST + 3 + a, lanes] = f[1][0:1]
                u = jnp.where(segment == 0, 0.0, u)
            gated[a * SEGMENTS : (a + 1) * SEGMENTS, lanes] = u
            for r in range(ORDER):
                held[r] = held[r] * decay[r] + u
        for r in range(ORDER):
            total = held[r]
            for i in range(3):
                fade = tables[FADE + i, r : r + 1, lanes]
                total = total + fade * pltpu.roll(total, 1 << i, 0)
            state[r : r + 1, lanes] = total[SEGMENTS - 1 :]

    by_group(channels, group)
    high = state[...].astype(BF16)
    message[0:ORDER, :] = high
    message[ORDER:EDGES, :] = (state[...] - high.astype(F32)).astype(BF16)
    edges[...] = jnp.zeros_like(edges)
    for s in range(2):
        edges[2 * s : 2 * s + 1, :] = streams[s, 0:1, :]
        edges[2 * s + 1 : 2 * s + 2, :] = streams[s, SEGMENTS : SEGMENTS + 1, :]
        edges[4 + 2 * s : 5 + 2 * s, :] = streams[s, span - SEGMENTS - 1 : span - SEGMENTS, :]
        edges[5 + 2 * s : 6 + 2 * s, :] = streams[s, span - 1 : span, :]
    row = lax.broadcasted_iota(jnp.int32, (8, LANES), 0)
    col = lax.broadcasted_iota(jnp.int32, (8, LANES), 1)
    pick = jnp.where(col == LANES - 2 + row, 1.0, 0.0).astype(BF16)
    edges[8:16, :] = lax.dot_general(pick, tail[...], NT, preferred_element_type=F32)
    message[EDGES:, :] = edges[...].astype(BF16)


def states(key_in, value_in, query_in, taps, damping, residue, skip):
    channels, span = key_in.shape
    shape = jax.ShapeDtypeStruct
    out = [
        shape((EDGES + 16, channels), BF16),
        shape((span, channels), F32),
        shape((16, channels), F32),
        shape((TABLES, ORDER, channels), F32),
    ]
    scratch = [
        pltpu.VMEM((2, channels, span), BF16),
        pltpu.VMEM((channels, LANES), BF16),
        pltpu.VMEM(taps.shape, F32),
        pltpu.VMEM(damping.shape, F32),
        pltpu.VMEM(residue.shape, F32),
        pltpu.VMEM(skip.shape, F32),
        pltpu.VMEM((2, span, channels), F32),
        pltpu.VMEM((ORDER, channels), F32),
        pltpu.VMEM((16, channels), F32),
        pltpu.SemaphoreType.DMA((7,)),
    ]
    return call(states_kernel, "states", out, scratch, outside=range(7))(
        key_in, value_in, query_in, taps, damping, residue, skip
    )


def local_kernel(
    gated, query_hbm, params, tables, after, local, gate, carry, reach, raw, stream, sem
):
    channels, span = query_hbm.shape
    steps = span // SEGMENTS
    copy = pltpu.make_async_copy(query_hbm, raw, sem)
    copy.start()
    order = order_matrix(span)
    copy.wait()
    stream[...] = lax.dot_general(order, raw[...], NT, preferred_element_type=F32)
    segment = segment_index()

    def group(lanes):
        taps = [params[6 + i : 7 + i, lanes] for i in range(3)]
        skip = params[SKIP : SKIP + 1, lanes]
        decay = [tables[DECAY, r : r + 1, lanes] for r in range(ORDER)]
        weight = [tables[WEIGHT, r : r + 1, lanes] for r in range(ORDER)]

        def at(a):
            if a >= 0:
                return stream[a * SEGMENTS : (a + 1) * SEGMENTS, lanes]
            rolled = pltpu.roll(at(a + steps), 1, 0)
            return jnp.where(segment == 0, 0.0, rolled)

        held = [jnp.zeros((SEGMENTS, LANES), F32) for _ in range(ORDER)]
        for a in range(steps):
            here = slice(a * SEGMENTS, (a + 1) * SEGMENTS)
            u = gated[here, lanes]
            parts = [skip * u, None, None, None]
            for r in range(ORDER):
                held[r] = held[r] * decay[r] + u
                term = weight[r] * held[r]
                parts[r % 4] = term if parts[r % 4] is None else parts[r % 4] + term
            local[here, lanes] = (parts[0] + parts[1]) + (parts[2] + parts[3])
            gate[here, lanes] = taps[0] * at(a) + taps[1] * at(a - 1) + taps[2] * at(a - 2)
        for r in range(ORDER):
            total = held[r]
            far = jnp.ones((SEGMENTS, LANES), F32)
            for i in range(3):
                fade = tables[FADE + i, r : r + 1, lanes]
                by = 1 << i
                total = total + jnp.where(segment < by, 0.0, fade * pltpu.roll(total, by, 0))
                far = jnp.where((segment & by) != 0, far * fade, far)
            total = jnp.where(segment < 1, 0.0, pltpu.roll(total, 1, 0))
            here = slice(r * SEGMENTS, (r + 1) * SEGMENTS)
            scale = weight[r] * decay[r]
            carry[here, lanes] = scale * total
            reach[here, lanes] = scale * far

    by_group(channels, group)


def local_scan(gated, query_in, params, tables, after):
    channels, span = query_in.shape
    shape = jax.ShapeDtypeStruct
    out = [
        shape((span, channels), F32),
        shape((span, channels), F32),
        shape((ORDER * SEGMENTS, channels), F32),
        shape((ORDER * SEGMENTS, channels), F32),
    ]
    scratch = [
        pltpu.VMEM((channels, span), BF16),
        pltpu.VMEM((span, channels), F32),
        pltpu.SemaphoreType.DMA,
    ]
    return call(local_kernel, "local_scan", out, scratch, outside=(1,), unread=(4,))(
        gated, query_in, params, tables, after
    )


def unpack(message):
    state = message[0:ORDER, :].astype(F32) + message[ORDER:EDGES, :].astype(F32)
    return state, message[EDGES:, :].astype(F32)


def gated_start(params, new, old):
    out = []
    for s in range(2):
        near, mid, far = (params[3 * s + i : 3 * s + i + 1, :] for i in range(3))
        first, second = new[2 * s : 2 * s + 1], new[2 * s + 1 : 2 * s + 2]
        before, last = old[4 + 2 * s : 5 + 2 * s], old[5 + 2 * s : 6 + 2 * s]
        out.append(
            (near * first + mid * last + far * before, near * second + mid * first + far * last)
        )
    (k0, k1), (v0, v1) = out
    return k0 * v0, k1 * v1


def merge_kernel(
    j, mine, theirs, before, border, params, tables, after, message, before_out, border_out
):
    size = STEPS[j][0]
    at = OVER_Z + 5 * j
    _, z = place_of()
    older = (z & size) != 0
    first = (z & (size - 1)) == 0
    my_state, my_edges = unpack(mine)
    state, edges = unpack(theirs)
    new = jnp.where(older, my_edges, edges)
    old = jnp.where(older, edges, my_edges)
    u0, u1 = gated_start(params, new, old)
    seam = tables[DECAY] * u0 + u1
    total = tables[at + 2] * state + tables[at + 3] * my_state + tables[at + 4] * seam
    high = total.astype(BF16)
    message[0:ORDER, :] = high
    message[ORDER:EDGES, :] = (total - high.astype(F32)).astype(BF16)
    row = lax.broadcasted_iota(jnp.int32, my_edges.shape, 0)
    message[EDGES:, :] = jnp.where(row < 4, old, new).astype(BF16)
    before_out[...] = before[...] + tables[at] * state + tables[at + 1] * seam
    border_out[...] = jnp.where(older & first, edges, border[...])


def merge(j, mine, theirs, before, border, params, tables, after):
    shape = jax.ShapeDtypeStruct
    out = [shape(mine.shape, BF16), shape(before.shape, F32), shape(border.shape, F32)]
    return call(functools.partial(merge_kernel, j), f"merge{j}", out, unread=(6,))(
        mine, theirs, before, border, params, tables, after
    )


def gate_kernel(
    mine,
    row1,
    row2,
    row3,
    before_in,
    border_in,
    local,
    gate,
    carry,
    reach,
    params,
    tables,
    out,
    before,
    starts,
):
    span, channels = local.shape
    steps = span // SEGMENTS
    y, z = place_of()
    rows = [unpack(m) for m in (mine, row1, row2, row3)]
    total = before_in[...]
    for s in range(3):
        u0, u1 = gated_start(params, rows[s][1], rows[s + 1][1])
        total = total + tables[OVER_Y + s] * rows[s + 1][0]
        total = total + tables[OVER_Y + 3 + s] * (tables[DECAY] * u0 + u1)
    border = jnp.where((z == 0) & (y >= 1), rows[1][1], border_in[...])
    u = [None, None]
    p = lambda i: params[i : i + 1, :]
    e = lambda i: border[4 + i : 5 + i]
    u[0] = (p(FIRST) + p(1) * e(1) + p(2) * e(0)) * (p(FIRST + 2) + p(4) * e(3) + p(5) * e(2))
    u[1] = (p(FIRST + 1) + p(2) * e(1)) * (p(FIRST + 3) + p(5) * e(3))
    before[...] = total + tables[GROWTH] * u[0] + tables[GROWTH + 1] * u[1]
    starts[0:1, :] = p(SKIP) * u[0] - p(GROWN) * u[1]
    starts[1:2, :] = p(SKIP) * u[1]
    starts[2:3, :] = p(7) * e(5) + p(8) * e(4)
    starts[3:4, :] = p(8) * e(5)
    segment = segment_index()

    def group(lanes):
        decay, term = [], []
        for r in range(ORDER):
            here = slice(r * SEGMENTS, (r + 1) * SEGMENTS)
            term.append(carry[here, lanes] + reach[here, lanes] * before[r : r + 1, lanes])
            decay.append(tables[DECAY, r : r + 1, lanes])
        for pair in range(steps // 2):
            both = []
            for a in (2 * pair, 2 * pair + 1):
                here = slice(a * SEGMENTS, (a + 1) * SEGMENTS)
                parts = [local[here, lanes], None, None, None]
                times = gate[here, lanes]
                if a < 2:
                    first = segment == 0
                    parts[0] = parts[0] + jnp.where(first, starts[a : a + 1, lanes], 0.0)
                    times = times + jnp.where(first, starts[2 + a : 3 + a, lanes], 0.0)
                for r in range(ORDER):
                    parts[r % 4] = term[r] if parts[r % 4] is None else parts[r % 4] + term[r]
                    term[r] = term[r] * decay[r]
                both.append(((parts[0] + parts[1]) + (parts[2] + parts[3])) * times)
            here = slice(pair * 2 * SEGMENTS, (pair + 1) * 2 * SEGMENTS)
            out[here, lanes] = jnp.concatenate(both, axis=0).astype(BF16)

    by_group(channels, group)


def gate_all(messages, before, border, local, gate, carry, reach, params, tables):
    out = jax.ShapeDtypeStruct(local.shape, BF16)
    scratch = [pltpu.VMEM(before.shape, F32), pltpu.VMEM((8, before.shape[1]), F32)]
    return call(gate_kernel, "gated", out, scratch)(
        *messages, before, border, local, gate, carry, reach, params, tables
    )


def blocks_kernel(weight_hbm, after, out, sems):
    columns = out.shape[1] // sems.shape[0]
    me = lax.axis_index("ch")
    copies = []
    for k in range(sems.shape[0]):
        at = pl.ds(pl.multiple_of((me ^ (2 * k)) * columns, columns), columns)
        copies.append(
            pltpu.make_async_copy(
                weight_hbm.at[:, at], out.at[:, k * columns : (k + 1) * columns], sems.at[k]
            )
        )
    for c in copies:
        c.start()
    for c in copies:
        c.wait()


def weight_blocks(weight, after):
    channels, width = weight.shape
    chips = lax.axis_size("ch") // 2
    out = jax.ShapeDtypeStruct((channels, width // 2), BF16)
    scratch = [pltpu.SemaphoreType.DMA((chips,))]
    return call(blocks_kernel, "weight_blocks", out, scratch, outside=(0,), unread=(1,))(weight, after)


def project(mine, other, weight, far, k, dtype):
    columns = far.shape[1] // lax.axis_size("ch")

    def kernel(mine_ref, other_ref, weight_ref, far_ref, out_ref):
        block = lax.axis_index("ch") ^ (2 * k)
        at = pl.ds(pl.multiple_of(block * columns, columns), columns)
        near = weight_ref[:, k * columns : (k + 1) * columns]
        total = jnp.dot(mine_ref[...], near, preferred_element_type=F32)
        total = total + jnp.dot(other_ref[...], far_ref[:, at], preferred_element_type=F32)
        out_ref[...] = total.astype(out_ref.dtype)

    out = jax.ShapeDtypeStruct((mine.shape[0], columns), dtype)
    return call(kernel, f"project{k}", out)(mine, other, weight, far)


def finish_kernel(own, a, b, c, out):
    total = own[...] + a[...].astype(F32)
    total = total + (b[...].astype(F32) + c[...].astype(F32))
    out[...] = lax.dot_general(
        total.astype(BF16), order_matrix(total.shape[0]), TN, preferred_element_type=F32
    ).astype(BF16)


def finish(own, received):
    span, columns = own.shape
    out = jax.ShapeDtypeStruct((columns, span), BF16)
    return call(finish_kernel, "finish", out, held=False)(own, *received)


def per_device(
    query_in, key_in, value_in, short_taps, modal_residue, mode_damping_speed, skip_gain, out_weight
):
    channels = query_in.shape[0]
    n_ctx, n_ch = lax.axis_size("ctx"), lax.axis_size("ch")
    sibling = [(i, i ^ 1) for i in range(n_ch)]
    far = lax.ppermute(out_weight, "ch", sibling)

    message, gated, params, tables = states(
        key_in,
        value_in,
        query_in,
        jnp.transpose(short_taps, (0, 2, 1)),
        mode_damping_speed.T,
        modal_residue.T,
        skip_gain[None, :],
    )
    before = jnp.zeros((ORDER, channels), F32)
    border = jnp.zeros((16, channels), F32)
    for j, (_, by) in enumerate(STEPS):
        theirs = lax.ppermute(message, "ctx", [(i, i ^ by) for i in range(n_ctx)])
        if j == 0:
            local, gate, carry, reach = local_scan(gated, query_in, params, tables, message)
            done = local
        if j == 1:
            done = weight = weight_blocks(out_weight, message)
        message, before, border = merge(j, message, theirs, before, border, params, tables, done)
    messages = [message]
    for s in range(1, n_ctx // ROW):
        pairs = [(i, i + s * ROW) for i in range(n_ctx - s * ROW)]
        messages.append(lax.ppermute(message, "ctx", pairs))

    own = gate_all(messages, before, border, local, gate, carry, reach, params, tables)
    other = lax.ppermute(own, "ch", sibling)
    received = []
    for k in (2, 1, 3):
        part = project(own, other, weight, far, k, BF16)
        received.append(lax.ppermute(part, "ch", [(i, i ^ (2 * k)) for i in range(n_ch)]))
    kept = project(own, other, weight, far, 0, F32)
    return finish(kept, received)


def solution(mesh):
    placed = (
        P("ch", "ctx"),
        P("ch", "ctx"),
        P("ch", "ctx"),
        P(None, "ch", None),
        P("ch", None),
        P("ch", None),
        P("ch"),
        P("ch", None),
    )
    return jax.shard_map(
        per_device, mesh=mesh, in_specs=placed, out_specs=P("ch", "ctx"), check_vma=False
    )
```

```python
import jax
import jax.numpy as jnp
from jax import lax
from jax.experimental import pallas as pl
from jax.experimental.pallas import tpu as pltpu
from jax.sharding import PartitionSpec as P

SEGMENTS = 8
LANES = 128
ORDER = 16
ROW = 8
SCOPED = 16 * 2**20
F32 = jnp.float32
BF16 = jnp.bfloat16
NT = (((1,), (1,)), ((), ()))
TN = (((0,), (0,)), ((), ()))

FOUR, PAIR = 4, 7
DECAY, FADE, WEIGHT, GROWTH = 0, 1, 4, 5
ALL, ALL_SEAM, AHEAD, AHEAD_SEAM, OVER_PAIR, OVER_Y = 7, 10, 13, 16, 18, 23
TABLES = 29
SKIP, GROWN, FIRST = 9, 10, 11
EDGES = 16


def call(kernel, name, out, scratch=(), held=True, outside=(), unread=()):
    whole = pl.BlockSpec(memory_space=pltpu.VMEM)
    place = (lambda o: pltpu.VMEM(o.shape, o.dtype)) if held else (lambda o: o)

    def run(*args):
        spaces = [
            pl.ANY if i in unread else pltpu.HBM if i in outside else pltpu.VMEM
            for i in range(len(args))
        ]
        return pl.pallas_call(
            kernel,
            in_specs=[pl.BlockSpec(memory_space=space) for space in spaces],
            out_specs=jax.tree.map(lambda _: whole, out),
            out_shape=jax.tree.map(place, out),
            scratch_shapes=list(scratch),
            compiler_params=pltpu.CompilerParams(vmem_limit_bytes=SCOPED),
            name=name,
        )(*(pltpu.with_memory_space_constraint(a, space) for a, space in zip(args, spaces)))

    return run


def order_matrix(span):
    steps = span // SEGMENTS
    row = lax.broadcasted_iota(jnp.int32, (span, span), 0)
    col = lax.broadcasted_iota(jnp.int32, (span, span), 1)
    return jnp.where(col == (row & (SEGMENTS - 1)) * steps + (row >> 3), 1.0, 0.0).astype(BF16)


def segment_index():
    return lax.broadcasted_iota(jnp.int32, (SEGMENTS, LANES), 0)


def by_group(channels, body):
    def step(g, nothing):
        body(pl.ds(pl.multiple_of(g * LANES, LANES), LANES))
        return nothing

    lax.fori_loop(0, channels // LANES, step, 0)


def place_of():
    here = lax.axis_index("ctx")
    return here // ROW, lax.rem(here, ROW)


def fill_tables(damping, residue, span, tables):
    y, z = place_of()

    def fade(by):
        return jnp.exp(-damping * by)

    def only(flag, value):
        return jnp.where(flag, value, 0.0)

    tables[DECAY] = fade(1.0)
    for i in range(3):
        tables[FADE + i] = fade(float((span // SEGMENTS) << i))
    tables[WEIGHT] = residue * jnp.sqrt(damping)
    tables[GROWTH] = fade(-1.0)
    tables[GROWTH + 1] = fade(-2.0)
    place = z & (FOUR - 1)
    for q in range(3):
        tables[ALL + q] = fade(float((3 - q) * span))
        tables[ALL_SEAM + q] = fade(float((3 - q) * span - 2))
        ahead = jnp.maximum(place - 1 - q, 0) * span
        tables[AHEAD + q] = only(q < place, fade(ahead.astype(F32)))
    for q in range(2):
        seen = jnp.maximum((place - 1 - q) * span - 2, 0)
        tables[AHEAD_SEAM + q] = only(q + 1 < place, fade(seen.astype(F32)))
    older = (z & FOUR) != 0
    ahead = place * span
    whole = fade(float(FOUR * span))
    tables[OVER_PAIR] = only(older, fade(ahead.astype(F32)))
    seen = jnp.maximum(ahead - 2, 0).astype(F32)
    tables[OVER_PAIR + 1] = only(older & (ahead > 0), fade(seen))
    tables[OVER_PAIR + 2] = jnp.where(older, whole, 1.0)
    tables[OVER_PAIR + 3] = jnp.where(older, 1.0, whole)
    tables[OVER_PAIR + 4] = fade(float(FOUR * span - 2))
    for s in range(3):
        ahead = (ROW * s + z) * span
        tables[OVER_Y + s] = only(y >= s + 1, fade(ahead.astype(F32)))
        seen = jnp.maximum(ahead - 2, 0).astype(F32)
        tables[OVER_Y + 3 + s] = only((y >= s + 1) & (ahead > 0), fade(seen))


def states_kernel(
    key_hbm,
    value_hbm,
    query_hbm,
    taps_hbm,
    damping_hbm,
    residue_hbm,
    skip_hbm,
    message,
    gated,
    params,
    tables,
    raw,
    tail,
    taps_in,
    damping,
    residue,
    skip,
    streams,
    state,
    edges,
    sems,
):
    channels, span = key_hbm.shape
    steps = span // SEGMENTS
    copies = [
        pltpu.make_async_copy(src, dst, sems.at[i])
        for i, (src, dst) in enumerate(
            (
                (damping_hbm, damping),
                (residue_hbm, residue),
                (key_hbm, raw.at[0]),
                (value_hbm, raw.at[1]),
                (taps_hbm, taps_in),
                (skip_hbm, skip),
                (query_hbm.at[:, span - LANES :], tail),
            )
        )
    ]
    for c in copies:
        c.start()
    order = order_matrix(span)
    for c in copies[:2]:
        c.wait()
    fill_tables(damping[...], residue[...], span, tables)
    for c in copies[2:]:
        c.wait()
    for s in range(2):
        streams[s] = lax.dot_general(order, raw[s], NT, preferred_element_type=F32)
    segment = segment_index()
    params[...] = jnp.zeros_like(params)
    for i in range(9):
        params[i : i + 1, :] = taps_in[(1 + i // 3) % 3, i % 3, :][None, :]
    params[SKIP : SKIP + 1, :] = skip[...]
    params[GROWN : GROWN + 1, :] = jnp.sum(
        tables[WEIGHT] * tables[GROWTH], axis=0, keepdims=True
    )

    def group(lanes):
        taps = [params[i : i + 1, lanes] for i in range(6)]
        decay = [tables[DECAY, r : r + 1, lanes] for r in range(ORDER)]

        def at(s, a):
            if a >= 0:
                return streams[s, a * SEGMENTS : (a + 1) * SEGMENTS, lanes]
            rolled = pltpu.roll(at(s, a + steps), 1, 0)
            return jnp.where(segment == 0, 0.0, rolled)

        held = [jnp.zeros((SEGMENTS, LANES), F32) for _ in range(ORDER)]
        for a in range(steps):
            f = [
                taps[3 * s] * at(s, a)
                + taps[3 * s + 1] * at(s, a - 1)
                + taps[3 * s + 2] * at(s, a - 2)
                for s in range(2)
            ]
            u = f[0] * f[1]
            if a < 2:
                params[FIRST + a : FIRST + a + 1, lanes] = f[0][0:1]
                params[FIRST + 2 + a : FIRST + 3 + a, lanes] = f[1][0:1]
                u = jnp.where(segment == 0, 0.0, u)
            gated[a * SEGMENTS : (a + 1) * SEGMENTS, lanes] = u
            for r in range(ORDER):
                held[r] = held[r] * decay[r] + u
        for r in range(ORDER):
            total = held[r]
            for i in range(3):
                fade = tables[FADE + i, r : r + 1, lanes]
                total = total + fade * pltpu.roll(total, 1 << i, 0)
            state[r : r + 1, lanes] = total[SEGMENTS - 1 :]

    by_group(channels, group)
    at = lambda i: params[FIRST + i : FIRST + i + 1, :]
    start_fade = jnp.exp(-damping[...] * float(span - 2))
    start = start_fade * (tables[DECAY] * (at(0) * at(2)) + at(1) * at(3))
    total = state[...] + jnp.where(lax.axis_index("ctx") == 0, start, 0.0)
    message[0:ORDER, :] = total.astype(BF16)
    edges[...] = jnp.zeros_like(edges)
    for s in range(2):
        edges[2 * s : 2 * s + 1, :] = streams[s, 0:1, :]
        edges[2 * s + 1 : 2 * s + 2, :] = streams[s, SEGMENTS : SEGMENTS + 1, :]
        edges[4 + 2 * s : 5 + 2 * s, :] = streams[s, span - SEGMENTS - 1 : span - SEGMENTS, :]
        edges[5 + 2 * s : 6 + 2 * s, :] = streams[s, span - 1 : span, :]
    row = lax.broadcasted_iota(jnp.int32, (8, LANES), 0)
    col = lax.broadcasted_iota(jnp.int32, (8, LANES), 1)
    pick = jnp.where(col == LANES - 2 + row, 1.0, 0.0).astype(BF16)
    edges[8:16, :] = lax.dot_general(pick, tail[...], NT, preferred_element_type=F32)
    message[EDGES:, :] = edges[...].astype(BF16)


def states(key_in, value_in, query_in, taps, damping, residue, skip):
    channels, span = key_in.shape
    shape = jax.ShapeDtypeStruct
    out = [
        shape((EDGES + 16, channels), BF16),
        shape((span, channels), F32),
        shape((16, channels), F32),
        shape((TABLES, ORDER, channels), F32),
    ]
    scratch = [
        pltpu.VMEM((2, channels, span), BF16),
        pltpu.VMEM((channels, LANES), BF16),
        pltpu.VMEM(taps.shape, F32),
        pltpu.VMEM(damping.shape, F32),
        pltpu.VMEM(residue.shape, F32),
        pltpu.VMEM(skip.shape, F32),
        pltpu.VMEM((2, span, channels), F32),
        pltpu.VMEM((ORDER, channels), F32),
        pltpu.VMEM((16, channels), F32),
        pltpu.SemaphoreType.DMA((7,)),
    ]
    return call(states_kernel, "states", out, scratch, outside=range(7))(
        key_in, value_in, query_in, taps, damping, residue, skip
    )


def local_kernel(
    gated, query_hbm, params, tables, after, local, gate, carry, reach, raw, stream, sem
):
    channels, span = query_hbm.shape
    steps = span // SEGMENTS
    copy = pltpu.make_async_copy(query_hbm, raw, sem)
    copy.start()
    order = order_matrix(span)
    copy.wait()
    stream[...] = lax.dot_general(order, raw[...], NT, preferred_element_type=F32)
    segment = segment_index()

    def group(lanes):
        taps = [params[6 + i : 7 + i, lanes] for i in range(3)]
        skip = params[SKIP : SKIP + 1, lanes]
        decay = [tables[DECAY, r : r + 1, lanes] for r in range(ORDER)]
        weight = [tables[WEIGHT, r : r + 1, lanes] for r in range(ORDER)]

        def at(a):
            if a >= 0:
                return stream[a * SEGMENTS : (a + 1) * SEGMENTS, lanes]
            rolled = pltpu.roll(at(a + steps), 1, 0)
            return jnp.where(segment == 0, 0.0, rolled)

        held = [jnp.zeros((SEGMENTS, LANES), F32) for _ in range(ORDER)]
        for a in range(steps):
            here = slice(a * SEGMENTS, (a + 1) * SEGMENTS)
            u = gated[here, lanes]
            parts = [skip * u, None, None, None]
            for r in range(ORDER):
                held[r] = held[r] * decay[r] + u
                term = weight[r] * held[r]
                parts[r % 4] = term if parts[r % 4] is None else parts[r % 4] + term
            local[here, lanes] = (parts[0] + parts[1]) + (parts[2] + parts[3])
            gate[here, lanes] = taps[0] * at(a) + taps[1] * at(a - 1) + taps[2] * at(a - 2)
        for r in range(ORDER):
            total = held[r]
            far = jnp.ones((SEGMENTS, LANES), F32)
            for i in range(3):
                fade = tables[FADE + i, r : r + 1, lanes]
                by = 1 << i
                total = total + jnp.where(segment < by, 0.0, fade * pltpu.roll(total, by, 0))
                far = jnp.where((segment & by) != 0, far * fade, far)
            total = jnp.where(segment < 1, 0.0, pltpu.roll(total, 1, 0))
            here = slice(r * SEGMENTS, (r + 1) * SEGMENTS)
            scale = weight[r] * decay[r]
            carry[here, lanes] = scale * total
            reach[here, lanes] = scale * far

    by_group(channels, group)


def local_scan(gated, query_in, params, tables, after):
    channels, span = query_in.shape
    shape = jax.ShapeDtypeStruct
    out = [
        shape((span, channels), F32),
        shape((span, channels), F32),
        shape((ORDER * SEGMENTS, channels), F32),
        shape((ORDER * SEGMENTS, channels), F32),
    ]
    scratch = [
        pltpu.VMEM((channels, span), BF16),
        pltpu.VMEM((span, channels), F32),
        pltpu.SemaphoreType.DMA,
    ]
    return call(local_kernel, "local_scan", out, scratch, outside=(1,), unread=(4,))(
        gated, query_in, params, tables, after
    )


def unpack(message):
    return message[0:ORDER, :].astype(F32), message[EDGES:, :].astype(F32)


def gated_start(params, new, old):
    out = []
    for s in range(2):
        near, mid, far = (params[3 * s + i : 3 * s + i + 1, :] for i in range(3))
        first, second = new[2 * s : 2 * s + 1], new[2 * s + 1 : 2 * s + 2]
        before, last = old[4 + 2 * s : 5 + 2 * s], old[5 + 2 * s : 6 + 2 * s]
        out.append(
            (near * first + mid * last + far * before, near * second + mid * first + far * last)
        )
    (k0, k1), (v0, v1) = out
    return k0 * v0, k1 * v1


def in_order(place, mine, swapped):
    one, two, three = swapped
    pick = lambda q, m, a, b, c: jnp.where(
        place == q, m, jnp.where((place ^ 1) == q, a, jnp.where((place ^ 2) == q, b, c))
    )
    return [
        tuple(pick(q, m, a, b, c) for m, a, b, c in zip(mine, one, two, three)) for q in range(4)
    ]


def send(message, state, first, last):
    message[0:ORDER, :] = state.astype(BF16)
    row = lax.broadcasted_iota(jnp.int32, first.shape, 0)
    message[EDGES:, :] = jnp.where(row < 4, first, last).astype(BF16)


def merge_four_kernel(mine, three, two, one, params, tables, after, message, before, border):
    _, z = place_of()
    place = z & (FOUR - 1)
    blocks = in_order(place, unpack(mine), [unpack(m) for m in (one, two, three)])
    total, ahead = blocks[3][0], jnp.zeros_like(before)
    for q in range(3):
        total = total + tables[ALL + q] * blocks[q][0]
        ahead = ahead + tables[AHEAD + q] * blocks[q][0]
        u0, u1 = gated_start(params, blocks[q + 1][1], blocks[q][1])
        seam = tables[DECAY] * u0 + u1
        total = total + tables[ALL_SEAM + q] * seam
        if q < 2:
            ahead = ahead + tables[AHEAD_SEAM + q] * seam
    send(message, total, blocks[0][1], blocks[3][1])
    before[...] = ahead
    last = jnp.zeros_like(border)
    for q in range(3):
        last = jnp.where(place == q + 1, blocks[q][1], last)
    border[...] = last


def merge_four(mine, swapped, params, tables, after):
    channels = mine.shape[1]
    shape = jax.ShapeDtypeStruct
    out = [shape(mine.shape, BF16), shape((ORDER, channels), F32), shape((16, channels), F32)]
    return call(merge_four_kernel, "merge_four", out, unread=(6,))(
        mine, *swapped, params, tables, after
    )


def merge_pair_kernel(
    mine, theirs, before, border, params, tables, after, message, before_out, border_out
):
    at = OVER_PAIR
    _, z = place_of()
    older = (z & FOUR) != 0
    first = (z & (FOUR - 1)) == 0
    my_state, my_edges = unpack(mine)
    state, edges = unpack(theirs)
    new = jnp.where(older, my_edges, edges)
    old = jnp.where(older, edges, my_edges)
    u0, u1 = gated_start(params, new, old)
    seam = tables[DECAY] * u0 + u1
    total = tables[at + 2] * state + tables[at + 3] * my_state + tables[at + 4] * seam
    send(message, total, old, new)
    before_out[...] = before[...] + tables[at] * state + tables[at + 1] * seam
    border_out[...] = jnp.where(older & first, edges, border[...])


def merge_pair(mine, theirs, before, border, params, tables, after):
    shape = jax.ShapeDtypeStruct
    out = [shape(mine.shape, BF16), shape(before.shape, F32), shape(border.shape, F32)]
    return call(merge_pair_kernel, "merge_pair", out, unread=(6,))(
        mine, theirs, before, border, params, tables, after
    )


def gate_kernel(
    mine,
    row3,
    row2,
    row1,
    before_in,
    border_in,
    local,
    gate,
    carry,
    reach,
    params,
    tables,
    out,
    before,
    starts,
):
    span, channels = local.shape
    steps = span // SEGMENTS
    y, z = place_of()
    lying = in_order(y, unpack(mine), [unpack(m) for m in (row1, row2, row3)])
    rows = [unpack(mine)]
    for s in range(1, 4):
        pick = lambda a, b, c: jnp.where(y - s == 0, a, jnp.where(y - s == 1, b, c))
        rows.append(tuple(pick(a, b, c) for a, b, c in zip(*lying[:3])))
    total = before_in[...]
    for s in range(3):
        u0, u1 = gated_start(params, rows[s][1], rows[s + 1][1])
        total = total + tables[OVER_Y + s] * rows[s + 1][0]
        total = total + tables[OVER_Y + 3 + s] * (tables[DECAY] * u0 + u1)
    border = jnp.where((z == 0) & (y >= 1), rows[1][1], border_in[...])
    u = [None, None]
    p = lambda i: params[i : i + 1, :]
    e = lambda i: border[4 + i : 5 + i]
    u[0] = (p(FIRST) + p(1) * e(1) + p(2) * e(0)) * (p(FIRST + 2) + p(4) * e(3) + p(5) * e(2))
    u[1] = (p(FIRST + 1) + p(2) * e(1)) * (p(FIRST + 3) + p(5) * e(3))
    before[...] = total + tables[GROWTH] * u[0] + tables[GROWTH + 1] * u[1]
    starts[0:1, :] = p(SKIP) * u[0] - p(GROWN) * u[1]
    starts[1:2, :] = p(SKIP) * u[1]
    starts[2:3, :] = p(7) * e(5) + p(8) * e(4)
    starts[3:4, :] = p(8) * e(5)
    segment = segment_index()

    def group(lanes):
        decay, term = [], []
        for r in range(ORDER):
            here = slice(r * SEGMENTS, (r + 1) * SEGMENTS)
            term.append(carry[here, lanes] + reach[here, lanes] * before[r : r + 1, lanes])
            decay.append(tables[DECAY, r : r + 1, lanes])
        for pair in range(steps // 2):
            both = []
            for a in (2 * pair, 2 * pair + 1):
                here = slice(a * SEGMENTS, (a + 1) * SEGMENTS)
                parts = [local[here, lanes], None, None, None]
                times = gate[here, lanes]
                if a < 2:
                    first = segment == 0
                    parts[0] = parts[0] + jnp.where(first, starts[a : a + 1, lanes], 0.0)
                    times = times + jnp.where(first, starts[2 + a : 3 + a, lanes], 0.0)
                for r in range(ORDER):
                    parts[r % 4] = term[r] if parts[r % 4] is None else parts[r % 4] + term[r]
                    term[r] = term[r] * decay[r]
                both.append(((parts[0] + parts[1]) + (parts[2] + parts[3])) * times)
            here = slice(pair * 2 * SEGMENTS, (pair + 1) * 2 * SEGMENTS)
            out[here, lanes] = jnp.concatenate(both, axis=0).astype(BF16)

    by_group(channels, group)


def gate_all(messages, before, border, local, gate, carry, reach, params, tables):
    out = jax.ShapeDtypeStruct(local.shape, BF16)
    scratch = [pltpu.VMEM(before.shape, F32), pltpu.VMEM((8, before.shape[1]), F32)]
    return call(gate_kernel, "gated", out, scratch)(
        *messages, before, border, local, gate, carry, reach, params, tables
    )


def blocks_kernel(weight_hbm, after, out, sems):
    columns = out.shape[1] // sems.shape[0]
    me = lax.axis_index("ch")
    copies = []
    for k in range(sems.shape[0]):
        at = pl.ds(pl.multiple_of((me ^ (2 * k)) * columns, columns), columns)
        copies.append(
            pltpu.make_async_copy(
                weight_hbm.at[:, at], out.at[:, k * columns : (k + 1) * columns], sems.at[k]
            )
        )
    for c in copies:
        c.start()
    for c in copies:
        c.wait()


def weight_blocks(weight, after):
    channels, width = weight.shape
    chips = lax.axis_size("ch") // 2
    out = jax.ShapeDtypeStruct((channels, width // 2), BF16)
    scratch = [pltpu.SemaphoreType.DMA((chips,))]
    return call(blocks_kernel, "weight_blocks", out, scratch, outside=(0,), unread=(1,))(weight, after)


def project(mine, other, weight, far, name, wanted, dtype):
    span = mine.shape[0]
    columns = far.shape[1] // lax.axis_size("ch")

    def kernel(mine_ref, other_ref, weight_ref, far_ref, *out_refs):
        for out_ref, (k, part) in zip(out_refs, wanted):
            block = lax.axis_index("ch") ^ (2 * k)
            there = pl.ds(pl.multiple_of(block * columns, columns), columns)
            here = slice(k * columns, (k + 1) * columns)
            rows = slice(None)
            if part is not None:
                rows = slice(part * (span // 2), (part + 1) * (span // 2))
            total = jnp.dot(mine_ref[rows, :], weight_ref[:, here], preferred_element_type=F32)
            total = total + jnp.dot(
                other_ref[rows, :], far_ref[:, there], preferred_element_type=F32
            )
            out_ref[...] = total.astype(out_ref.dtype)

    out = [
        jax.ShapeDtypeStruct((span if part is None else span // 2, columns), dtype)
        for _, part in wanted
    ]
    return call(kernel, name, out)(mine, other, weight, far)


def relay_kernel(passing, own, out):
    out[...] = (passing[...].astype(F32) + own[...]).astype(BF16)


def relay(passing, own):
    return call(relay_kernel, "relay", jax.ShapeDtypeStruct(own.shape, BF16))(passing, own)


def finish_kernel(own, direct1, joined3, direct3, joined1, out):
    half = direct1.shape[0]
    top = own[0:half, :] + (direct1[...].astype(F32) + joined3[...].astype(F32))
    low = own[half:, :] + (direct3[...].astype(F32) + joined1[...].astype(F32))
    total = jnp.concatenate([top.astype(BF16), low.astype(BF16)], axis=0)
    out[...] = lax.dot_general(
        total, order_matrix(total.shape[0]), TN, preferred_element_type=F32
    ).astype(BF16)


def finish(own, *received):
    span, columns = own.shape
    out = jax.ShapeDtypeStruct((columns, span), BF16)
    return call(finish_kernel, "finish", out, held=False)(own, *received)


def per_device(
    query_in, key_in, value_in, short_taps, modal_residue, mode_damping_speed, skip_gain, out_weight
):
    channels = query_in.shape[0]
    n_ctx, n_ch = lax.axis_size("ctx"), lax.axis_size("ch")
    sibling = [(i, i ^ 1) for i in range(n_ch)]
    far = lax.ppermute(out_weight, "ch", sibling)

    message, gated, params, tables = states(
        key_in,
        value_in,
        query_in,
        jnp.transpose(short_taps, (0, 2, 1)),
        mode_damping_speed.T,
        modal_residue.T,
        skip_gain[None, :],
    )
    def across(value, by):
        return lax.ppermute(value, "ctx", [(i, i ^ by) for i in range(n_ctx)])

    swapped = [across(message, k) for k in (3, 2, 1)]
    local, gate, carry, reach = local_scan(gated, query_in, params, tables, message)
    message, before, border = merge_four(message, swapped, params, tables, local)
    theirs = across(message, PAIR)
    weight = weight_blocks(out_weight, message)
    message, before, border = merge_pair(message, theirs, before, border, params, tables, weight)
    messages = [message] + [across(message, k * ROW) for k in (3, 2, 1)]

    own = gate_all(messages, before, border, local, gate, carry, reach, params, tables)
    other = lax.ppermute(own, "ch", sibling)

    def swap(value, k):
        return lax.ppermute(value, "ch", [(i, i ^ (2 * k)) for i in range(n_ch)])

    operands = (own, other, weight, far)
    over3, over1 = project(*operands, "opposite", [(2, 1), (2, 0)], BF16)
    over3, over1 = swap(over3, 3), swap(over1, 1)
    direct3, direct1 = project(*operands, "neighbours", [(3, 1), (1, 0)], BF16)
    direct3, direct1 = swap(direct3, 3), swap(direct1, 1)
    mine3, mine1 = project(*operands, "joining", [(3, 0), (1, 1)], F32)
    (kept,) = project(*operands, "kept", [(0, None)], F32)
    joined1 = swap(relay(over3, mine1), 1)
    joined3 = swap(relay(over1, mine3), 3)
    return finish(kept, direct1, joined3, direct3, joined1)


def solution(mesh):
    placed = (
        P("ch", "ctx"),
        P("ch", "ctx"),
        P("ch", "ctx"),
        P(None, "ch", None),
        P("ch", None),
        P("ch", None),
        P("ch"),
        P("ch", None),
    )
    return jax.shard_map(
        per_device, mesh=mesh, in_specs=placed, out_specs=P("ch", "ctx"), check_vma=False
    )
```

```python
import jax
import jax.numpy as jnp
from jax import lax
from jax.experimental import pallas as pl
from jax.experimental.pallas import tpu as pltpu
from jax.sharding import PartitionSpec as P

SEGMENTS = 8
LANES = 128
ORDER = 16
ROW = 8
SCOPED = 16 * 2**20
F32 = jnp.float32
BF16 = jnp.bfloat16
NT = (((1,), (1,)), ((), ()))
TN = (((0,), (0,)), ((), ()))

FOUR, PAIR = 4, 7
DECAY, FADE, WEIGHT, GROWTH = 0, 1, 4, 5
ALL, ALL_SEAM, AHEAD, AHEAD_SEAM, OVER_PAIR, OVER_Y = 7, 10, 13, 16, 18, 23
TABLES = 29
SKIP, FIRST = 9, 10
EDGES = 16


def call(kernel, name, out, scratch=(), held=True, outside=(), unread=()):
    whole = pl.BlockSpec(memory_space=pltpu.VMEM)
    if not held:
        whole = pl.BlockSpec(memory_space=pl.ANY)
    place = (lambda o: pltpu.VMEM(o.shape, o.dtype)) if held else (lambda o: o)

    def run(*args):
        spaces = [
            pl.ANY if i in unread else pltpu.HBM if i in outside else pltpu.VMEM
            for i in range(len(args))
        ]
        return pl.pallas_call(
            kernel,
            in_specs=[pl.BlockSpec(memory_space=space) for space in spaces],
            out_specs=jax.tree.map(lambda _: whole, out),
            out_shape=jax.tree.map(place, out),
            scratch_shapes=list(scratch),
            compiler_params=pltpu.CompilerParams(vmem_limit_bytes=SCOPED),
            name=name,
        )(*(pltpu.with_memory_space_constraint(a, space) for a, space in zip(args, spaces)))

    return run


def order_matrix(span):
    steps = span // SEGMENTS
    row = lax.broadcasted_iota(jnp.int32, (span, span), 0)
    col = lax.broadcasted_iota(jnp.int32, (span, span), 1)
    return jnp.where(col == (row & (SEGMENTS - 1)) * steps + (row >> 3), 1.0, 0.0).astype(BF16)


def segment_index():
    return lax.broadcasted_iota(jnp.int32, (SEGMENTS, LANES), 0)


def by_group(channels, body):
    def step(g, nothing):
        body(pl.ds(pl.multiple_of(g * LANES, LANES), LANES))
        return nothing

    lax.fori_loop(0, channels // LANES, step, 0)


def place_of():
    here = lax.axis_index("ctx")
    return here // ROW, lax.rem(here, ROW)


def fill_tables(basis, modes, span, tables):
    y, z = place_of()
    damping, residue = modes[0], modes[1]

    def fade(by):
        return jnp.exp(-damping * by)

    def only(flag, value):
        return jnp.where(flag, value, 0.0)

    for i in range(4):
        tables[DECAY + i] = basis[i]
    tables[WEIGHT] = residue * jnp.sqrt(damping)
    tables[GROWTH] = fade(-1.0)
    tables[GROWTH + 1] = fade(-2.0)
    place = z & (FOUR - 1)
    for q in range(3):
        tables[ALL + q] = fade(float((3 - q) * span))
        tables[ALL_SEAM + q] = fade(float((3 - q) * span - 2))
        ahead = jnp.maximum(place - 1 - q, 0) * span
        tables[AHEAD + q] = only(q < place, fade(ahead.astype(F32)))
    for q in range(2):
        seen = jnp.maximum((place - 1 - q) * span - 2, 0)
        tables[AHEAD_SEAM + q] = only(q + 1 < place, fade(seen.astype(F32)))
    older = (z & FOUR) != 0
    ahead = place * span
    whole = fade(float(FOUR * span))
    tables[OVER_PAIR] = only(older, fade(ahead.astype(F32)))
    seen = jnp.maximum(ahead - 2, 0).astype(F32)
    tables[OVER_PAIR + 1] = only(older & (ahead > 0), fade(seen))
    tables[OVER_PAIR + 2] = jnp.where(older, whole, 1.0)
    tables[OVER_PAIR + 3] = jnp.where(older, 1.0, whole)
    tables[OVER_PAIR + 4] = fade(float(FOUR * span - 2))
    for s in range(3):
        ahead = (ROW * s + z) * span
        tables[OVER_Y + s] = only(y >= s + 1, fade(ahead.astype(F32)))
        seen = jnp.maximum(ahead - 2, 0).astype(F32)
        tables[OVER_Y + 3 + s] = only((y >= s + 1) & (ahead > 0), fade(seen))


def states_kernel(
    key_hbm,
    value_hbm,
    query_hbm,
    taps_hbm,
    damping_hbm,
    residue_hbm,
    skip_hbm,
    message,
    gated,
    params,
    basis,
    modes,
    order,
    raw,
    tail,
    taps_in,
    skip,
    streams,
    state,
    edges,
    sems,
):
    channels, span = key_hbm.shape
    steps = span // SEGMENTS
    fixed = [
        pltpu.make_async_copy(src, dst, sems.at[i])
        for i, (src, dst) in enumerate(
            (
                (damping_hbm, modes.at[0]),
                (taps_hbm, taps_in),
                (residue_hbm, modes.at[1]),
                (skip_hbm, skip),
                (query_hbm.at[:, span - LANES :], tail),
            )
        )
    ]

    big = [
        pltpu.make_async_copy(src, raw.at[s], sems.at[len(fixed) + s])
        for s, src in enumerate((key_hbm, value_hbm))
    ]
    for c in fixed[:2]:
        c.start()
    for c in big:
        c.start()
    for c in fixed[2:]:
        c.start()
    order[...] = order_matrix(span)
    segment = segment_index()
    params[...] = jnp.zeros_like(params)
    edges[...] = jnp.zeros_like(edges)
    for c in fixed[:2]:
        c.wait()
    basis[DECAY] = jnp.exp(-modes[0])
    for i in range(3):
        basis[FADE + i] = jnp.exp(-modes[0] * float(steps << i))
    for i in range(9):
        params[i : i + 1, :] = taps_in[(1 + i // 3) % 3, i % 3, :][None, :]
    for s in range(2):
        big[s].wait()
        streams[s] = lax.dot_general(order[...], raw[s], NT, preferred_element_type=F32)

    def group(lanes):
        taps = [params[i : i + 1, lanes] for i in range(6)]
        decay = [basis[DECAY, r : r + 1, lanes] for r in range(ORDER)]

        def at(s, a):
            if a >= 0:
                return streams[s, a * SEGMENTS : (a + 1) * SEGMENTS, lanes]
            rolled = pltpu.roll(at(s, a + steps), 1, 0)
            return jnp.where(segment == 0, 0.0, rolled)

        held = [jnp.zeros((SEGMENTS, LANES), F32) for _ in range(ORDER)]
        for a in range(steps):
            f = [
                taps[3 * s] * at(s, a)
                + taps[3 * s + 1] * at(s, a - 1)
                + taps[3 * s + 2] * at(s, a - 2)
                for s in range(2)
            ]
            u = f[0] * f[1]
            if a < 2:
                params[FIRST + a : FIRST + a + 1, lanes] = f[0][0:1]
                params[FIRST + 2 + a : FIRST + 3 + a, lanes] = f[1][0:1]
                u = jnp.where(segment == 0, 0.0, u)
            gated[a * SEGMENTS : (a + 1) * SEGMENTS, lanes] = u
            for r in range(ORDER):
                held[r] = held[r] * decay[r] + u
        for r in range(ORDER):
            total = held[r]
            for i in range(3):
                fade = basis[FADE + i, r : r + 1, lanes]
                total = total + fade * pltpu.roll(total, 1 << i, 0)
            state[r : r + 1, lanes] = total[SEGMENTS - 1 :]

    by_group(channels, group)
    at = lambda i: params[FIRST + i : FIRST + i + 1, :]
    start_fade = jnp.exp(-modes[0] * float(span - 2))
    start = start_fade * (basis[DECAY] * (at(0) * at(2)) + at(1) * at(3))
    total = state[...] + jnp.where(lax.axis_index("ctx") == 0, start, 0.0)
    message[0:ORDER, :] = total.astype(BF16)
    for c in fixed[2:]:
        c.wait()
    params[SKIP : SKIP + 1, :] = skip[...]
    for s in range(2):
        edges[2 * s : 2 * s + 1, :] = streams[s, 0:1, :]
        edges[2 * s + 1 : 2 * s + 2, :] = streams[s, SEGMENTS : SEGMENTS + 1, :]
        edges[4 + 2 * s : 5 + 2 * s, :] = streams[s, span - SEGMENTS - 1 : span - SEGMENTS, :]
        edges[5 + 2 * s : 6 + 2 * s, :] = streams[s, span - 1 : span, :]
    row = lax.broadcasted_iota(jnp.int32, (8, LANES), 0)
    col = lax.broadcasted_iota(jnp.int32, (8, LANES), 1)
    pick = jnp.where(col == LANES - 2 + row, 1.0, 0.0).astype(BF16)
    edges[8:16, :] = lax.dot_general(pick, tail[...], NT, preferred_element_type=F32)
    message[EDGES:, :] = edges[...].astype(BF16)


def states(key_in, value_in, query_in, taps, damping, residue, skip):
    channels, span = key_in.shape
    shape = jax.ShapeDtypeStruct
    out = [
        shape((EDGES + 16, channels), BF16),
        shape((span, channels), F32),
        shape((16, channels), F32),
        shape((4, ORDER, channels), F32),
        shape((2, ORDER, channels), F32),
        shape((span, span), BF16),
    ]
    scratch = [
        pltpu.VMEM((2, channels, span), BF16),
        pltpu.VMEM((channels, LANES), BF16),
        pltpu.VMEM(taps.shape, F32),
        pltpu.VMEM(skip.shape, F32),
        pltpu.VMEM((2, span, channels), F32),
        pltpu.VMEM((ORDER, channels), F32),
        pltpu.VMEM((16, channels), F32),
        pltpu.SemaphoreType.DMA((7,)),
    ]
    return call(states_kernel, "states", out, scratch, outside=range(7))(
        key_in, value_in, query_in, taps, damping, residue, skip
    )


def local_kernel(
    gated,
    query_hbm,
    params,
    basis,
    modes,
    order,
    after,
    local,
    gate,
    carry,
    reach,
    tables,
    raw,
    stream,
    sem,
):
    channels, span = query_hbm.shape
    steps = span // SEGMENTS
    copy = pltpu.make_async_copy(query_hbm, raw, sem)
    copy.start()
    fill_tables(basis, modes, span, tables)
    copy.wait()
    stream[...] = lax.dot_general(order[...], raw[...], NT, preferred_element_type=F32)
    segment = segment_index()

    def group(lanes):
        taps = [params[6 + i : 7 + i, lanes] for i in range(3)]
        skip = params[SKIP : SKIP + 1, lanes]
        decay = [tables[DECAY, r : r + 1, lanes] for r in range(ORDER)]
        weight = [tables[WEIGHT, r : r + 1, lanes] for r in range(ORDER)]

        def at(a):
            if a >= 0:
                return stream[a * SEGMENTS : (a + 1) * SEGMENTS, lanes]
            rolled = pltpu.roll(at(a + steps), 1, 0)
            return jnp.where(segment == 0, 0.0, rolled)

        held = [jnp.zeros((SEGMENTS, LANES), F32) for _ in range(ORDER)]
        for a in range(steps):
            here = slice(a * SEGMENTS, (a + 1) * SEGMENTS)
            u = gated[here, lanes]
            parts = [skip * u, None, None, None]
            for r in range(ORDER):
                held[r] = held[r] * decay[r] + u
                term = weight[r] * held[r]
                parts[r % 4] = term if parts[r % 4] is None else parts[r % 4] + term
            local[here, lanes] = (parts[0] + parts[1]) + (parts[2] + parts[3])
            gate[here, lanes] = taps[0] * at(a) + taps[1] * at(a - 1) + taps[2] * at(a - 2)
        for r in range(ORDER):
            total = held[r]
            far = jnp.ones((SEGMENTS, LANES), F32)
            for i in range(3):
                fade = tables[FADE + i, r : r + 1, lanes]
                by = 1 << i
                total = total + jnp.where(segment < by, 0.0, fade * pltpu.roll(total, by, 0))
                far = jnp.where((segment & by) != 0, far * fade, far)
            total = jnp.where(segment < 1, 0.0, pltpu.roll(total, 1, 0))
            here = slice(r * SEGMENTS, (r + 1) * SEGMENTS)
            scale = weight[r] * decay[r]
            carry[here, lanes] = scale * total
            reach[here, lanes] = scale * far

    by_group(channels, group)


def local_scan(gated, query_in, params, basis, modes, order, after):
    channels, span = query_in.shape
    shape = jax.ShapeDtypeStruct
    out = [
        shape((span, channels), F32),
        shape((span, channels), F32),
        shape((ORDER * SEGMENTS, channels), F32),
        shape((ORDER * SEGMENTS, channels), F32),
        shape((TABLES, ORDER, channels), F32),
    ]
    scratch = [
        pltpu.VMEM((channels, span), BF16),
        pltpu.VMEM((span, channels), F32),
        pltpu.SemaphoreType.DMA,
    ]
    return call(local_kernel, "local_scan", out, scratch, outside=(1,), unread=(6,))(
        gated, query_in, params, basis, modes, order, after
    )


def unpack(message):
    return message[0:ORDER, :].astype(F32), message[EDGES:, :].astype(F32)


def gated_start(params, new, old):
    out = []
    for s in range(2):
        near, mid, far = (params[3 * s + i : 3 * s + i + 1, :] for i in range(3))
        first, second = new[2 * s : 2 * s + 1], new[2 * s + 1 : 2 * s + 2]
        before, last = old[4 + 2 * s : 5 + 2 * s], old[5 + 2 * s : 6 + 2 * s]
        out.append(
            (near * first + mid * last + far * before, near * second + mid * first + far * last)
        )
    (k0, k1), (v0, v1) = out
    return k0 * v0, k1 * v1


def in_order(place, mine, swapped):
    one, two, three = swapped
    pick = lambda q, m, a, b, c: jnp.where(
        place == q, m, jnp.where((place ^ 1) == q, a, jnp.where((place ^ 2) == q, b, c))
    )
    return [
        tuple(pick(q, m, a, b, c) for m, a, b, c in zip(mine, one, two, three)) for q in range(4)
    ]


def send(message, state, first, last):
    message[0:ORDER, :] = state.astype(BF16)
    row = lax.broadcasted_iota(jnp.int32, first.shape, 0)
    message[EDGES:, :] = jnp.where(row < 4, first, last).astype(BF16)


def merge_four_kernel(mine, three, two, one, params, tables, after, message, before, border):
    _, z = place_of()
    place = z & (FOUR - 1)
    blocks = in_order(place, unpack(mine), [unpack(m) for m in (one, two, three)])
    total, ahead = blocks[3][0], jnp.zeros_like(before)
    for q in range(3):
        total = total + tables[ALL + q] * blocks[q][0]
        ahead = ahead + tables[AHEAD + q] * blocks[q][0]
        u0, u1 = gated_start(params, blocks[q + 1][1], blocks[q][1])
        seam = tables[DECAY] * u0 + u1
        total = total + tables[ALL_SEAM + q] * seam
        if q < 2:
            ahead = ahead + tables[AHEAD_SEAM + q] * seam
    send(message, total, blocks[0][1], blocks[3][1])
    before[...] = ahead
    last = jnp.zeros_like(border)
    for q in range(3):
        last = jnp.where(place == q + 1, blocks[q][1], last)
    border[...] = last


def merge_four(mine, swapped, params, tables, after):
    channels = mine.shape[1]
    shape = jax.ShapeDtypeStruct
    out = [shape(mine.shape, BF16), shape((ORDER, channels), F32), shape((16, channels), F32)]
    return call(merge_four_kernel, "merge_four", out, unread=(6,))(
        mine, *swapped, params, tables, after
    )


def merge_pair_kernel(
    mine, theirs, before, border, params, tables, after, message, before_out, border_out
):
    at = OVER_PAIR
    _, z = place_of()
    older = (z & FOUR) != 0
    first = (z & (FOUR - 1)) == 0
    my_state, my_edges = unpack(mine)
    state, edges = unpack(theirs)
    new = jnp.where(older, my_edges, edges)
    old = jnp.where(older, edges, my_edges)
    u0, u1 = gated_start(params, new, old)
    seam = tables[DECAY] * u0 + u1
    total = tables[at + 2] * state + tables[at + 3] * my_state + tables[at + 4] * seam
    send(message, total, old, new)
    before_out[...] = before[...] + tables[at] * state + tables[at + 1] * seam
    border_out[...] = jnp.where(older & first, edges, border[...])


def merge_pair(mine, theirs, before, border, params, tables, after):
    shape = jax.ShapeDtypeStruct
    out = [shape(mine.shape, BF16), shape(before.shape, F32), shape(border.shape, F32)]
    return call(merge_pair_kernel, "merge_pair", out, unread=(6,))(
        mine, theirs, before, border, params, tables, after
    )


def gate_kernel(
    mine,
    row3,
    row2,
    row1,
    before_in,
    border_in,
    local,
    gate,
    carry,
    reach,
    params,
    tables,
    out,
    before,
    starts,
):
    span, channels = local.shape
    steps = span // SEGMENTS
    y, z = place_of()
    lying = in_order(y, unpack(mine), [unpack(m) for m in (row1, row2, row3)])
    rows = [unpack(mine)]
    for s in range(1, 4):
        pick = lambda a, b, c: jnp.where(y - s == 0, a, jnp.where(y - s == 1, b, c))
        rows.append(tuple(pick(a, b, c) for a, b, c in zip(*lying[:3])))
    total = before_in[...]
    for s in range(3):
        u0, u1 = gated_start(params, rows[s][1], rows[s + 1][1])
        total = total + tables[OVER_Y + s] * rows[s + 1][0]
        total = total + tables[OVER_Y + 3 + s] * (tables[DECAY] * u0 + u1)
    border = jnp.where((z == 0) & (y >= 1), rows[1][1], border_in[...])
    u = [None, None]
    p = lambda i: params[i : i + 1, :]
    e = lambda i: border[4 + i : 5 + i]
    u[0] = (p(FIRST) + p(1) * e(1) + p(2) * e(0)) * (p(FIRST + 2) + p(4) * e(3) + p(5) * e(2))
    u[1] = (p(FIRST + 1) + p(2) * e(1)) * (p(FIRST + 3) + p(5) * e(3))
    before[...] = total + tables[GROWTH] * u[0] + tables[GROWTH + 1] * u[1]
    grown = jnp.sum(tables[WEIGHT] * tables[GROWTH], axis=0, keepdims=True)
    starts[0:1, :] = p(SKIP) * u[0] - grown * u[1]
    starts[1:2, :] = p(SKIP) * u[1]
    starts[2:3, :] = p(7) * e(5) + p(8) * e(4)
    starts[3:4, :] = p(8) * e(5)
    segment = segment_index()

    def group(lanes):
        decay, term = [], []
        for r in range(ORDER):
            here = slice(r * SEGMENTS, (r + 1) * SEGMENTS)
            term.append(carry[here, lanes] + reach[here, lanes] * before[r : r + 1, lanes])
            decay.append(tables[DECAY, r : r + 1, lanes])
        for pair in range(steps // 2):
            both = []
            for a in (2 * pair, 2 * pair + 1):
                here = slice(a * SEGMENTS, (a + 1) * SEGMENTS)
                parts = [local[here, lanes], None, None, None]
                times = gate[here, lanes]
                if a < 2:
                    first = segment == 0
                    parts[0] = parts[0] + jnp.where(first, starts[a : a + 1, lanes], 0.0)
                    times = times + jnp.where(first, starts[2 + a : 3 + a, lanes], 0.0)
                for r in range(ORDER):
                    parts[r % 4] = term[r] if parts[r % 4] is None else parts[r % 4] + term[r]
                    term[r] = term[r] * decay[r]
                both.append(((parts[0] + parts[1]) + (parts[2] + parts[3])) * times)
            here = slice(pair * 2 * SEGMENTS, (pair + 1) * 2 * SEGMENTS)
            out[here, lanes] = jnp.concatenate(both, axis=0).astype(BF16)

    by_group(channels, group)


def gate_all(messages, before, border, local, gate, carry, reach, params, tables):
    out = jax.ShapeDtypeStruct(local.shape, BF16)
    scratch = [pltpu.VMEM(before.shape, F32), pltpu.VMEM((8, before.shape[1]), F32)]
    return call(gate_kernel, "gated", out, scratch)(
        *messages, before, border, local, gate, carry, reach, params, tables
    )


def blocks_kernel(weight_hbm, after, out, sems):
    columns = out.shape[1] // sems.shape[0]
    me = lax.axis_index("ch")
    copies = []
    for k in range(sems.shape[0]):
        at = pl.ds(pl.multiple_of((me ^ (2 * k)) * columns, columns), columns)
        copies.append(
            pltpu.make_async_copy(
                weight_hbm.at[:, at], out.at[:, k * columns : (k + 1) * columns], sems.at[k]
            )
        )
    for c in copies:
        c.start()
    for c in copies:
        c.wait()


def weight_blocks(weight, after):
    channels, width = weight.shape
    chips = lax.axis_size("ch") // 2
    out = jax.ShapeDtypeStruct((channels, width // 2), BF16)
    scratch = [pltpu.SemaphoreType.DMA((chips,))]
    return call(blocks_kernel, "weight_blocks", out, scratch, outside=(0,), unread=(1,))(weight, after)


def near_kernel(mine, weight, out):
    out[...] = jnp.dot(mine[...], weight[...], preferred_element_type=F32)


def near_sums(mine, weight):
    out = jax.ShapeDtypeStruct((mine.shape[0], weight.shape[1]), F32)
    return call(near_kernel, "near_sums", out)(mine, weight)


def project(near, other, far, name, wanted, dtype):
    span = near.shape[0]
    half = span // 2
    columns = far.shape[1] // lax.axis_size("ch")

    def kernel(near_ref, other_ref, far_ref, *out_refs):
        for out_ref, parts in zip(out_refs, wanted):
            for i, (k, part) in enumerate(parts):
                block = lax.axis_index("ch") ^ (2 * k)
                there = pl.ds(pl.multiple_of(block * columns, columns), columns)
                rows = slice(part * half, (part + 1) * half)
                total = near_ref[rows, k * columns : (k + 1) * columns] + jnp.dot(
                    other_ref[rows, :], far_ref[:, there], preferred_element_type=F32
                )
                out_ref[i * half : (i + 1) * half, :] = total.astype(dtype)

    out = [jax.ShapeDtypeStruct((half * len(parts), columns), dtype) for parts in wanted]
    return call(kernel, name, out)(near, other, far)


def relay_kernel(passing, own, out):
    out[...] = (passing[...].astype(F32) + own[...]).astype(BF16)


def relay(passing, own):
    return call(relay_kernel, "relay", jax.ShapeDtypeStruct(own.shape, BF16))(passing, own)


def finish_kernel(own, direct1, direct3, joined1, joined3, order, out, result, sems):
    half = joined1.shape[0]
    columns = own.shape[1]
    copies = []
    for i in range(2):
        here = slice(i * columns // 2, (i + 1) * columns // 2)
        top = own[0:half, here] + (direct1[:, here].astype(F32) + joined3[:, here].astype(F32))
        low = own[half:, here] + (direct3[:, here].astype(F32) + joined1[:, here].astype(F32))
        total = jnp.concatenate([top.astype(BF16), low.astype(BF16)], axis=0)
        result[here, :] = lax.dot_general(
            total, order[...], TN, preferred_element_type=F32
        ).astype(BF16)
        copies.append(pltpu.make_async_copy(result.at[here, :], out.at[here, :], sems.at[i]))
        copies[-1].start()
    for c in copies:
        c.wait()


def finish(own, *received):
    span, columns = own.shape
    out = jax.ShapeDtypeStruct((columns, span), BF16)
    scratch = [pltpu.VMEM(out.shape, BF16), pltpu.SemaphoreType.DMA((2,))]
    return call(finish_kernel, "finish", out, scratch, held=False)(own, *received)


def per_device(
    query_in, key_in, value_in, short_taps, modal_residue, mode_damping_speed, skip_gain, out_weight
):
    channels = query_in.shape[0]
    n_ctx, n_ch = lax.axis_size("ctx"), lax.axis_size("ch")
    sibling = [(i, i ^ 1) for i in range(n_ch)]
    message, gated, params, basis, modes, order = states(
        key_in,
        value_in,
        query_in,
        jnp.transpose(short_taps, (0, 2, 1)),
        mode_damping_speed.T,
        modal_residue.T,
        skip_gain[None, :],
    )
    def across(value, by):
        return lax.ppermute(value, "ctx", [(i, i ^ by) for i in range(n_ctx)])

    swapped = [across(message, k) for k in (3, 2, 1)]
    local, gate, carry, reach, tables = local_scan(
        gated, query_in, params, basis, modes, order, message
    )
    message, before, border = merge_four(message, swapped, params, tables, local)
    later, _ = lax.optimization_barrier((out_weight, message))
    far = lax.ppermute(later, "ch", sibling)
    theirs = across(message, PAIR)
    weight = weight_blocks(out_weight, message)
    message, before, border = merge_pair(message, theirs, before, border, params, tables, weight)
    messages = [message] + [across(message, k * ROW) for k in (3, 2, 1)]

    own = gate_all(messages, before, border, local, gate, carry, reach, params, tables)
    other = lax.ppermute(own, "ch", sibling)

    def swap(value, k):
        return lax.ppermute(value, "ch", [(i, i ^ (2 * k)) for i in range(n_ch)])

    operands = (near_sums(own, weight), other, far)
    over3, over1 = project(*operands, "opposite", [[(2, 1)], [(2, 0)]], BF16)
    over3, over1 = swap(over3, 3), swap(over1, 1)
    direct3, direct1 = project(*operands, "neighbours", [[(3, 1)], [(1, 0)]], BF16)
    direct3, direct1 = swap(direct3, 3), swap(direct1, 1)
    mine3, mine1 = project(*operands, "joining", [[(3, 0)], [(1, 1)]], F32)
    (kept,) = project(*operands, "kept", [[(0, 0), (0, 1)]], F32)
    joined1 = swap(relay(over3, mine1), 1)
    joined3 = swap(relay(over1, mine3), 3)
    return finish(kept, direct1, direct3, joined1, joined3, order)


def solution(mesh):
    placed = (
        P("ch", "ctx"),
        P("ch", "ctx"),
        P("ch", "ctx"),
        P(None, "ch", None),
        P("ch", None),
        P("ch", None),
        P("ch"),
        P("ch", None),
    )
    return jax.shard_map(
        per_device, mesh=mesh, in_specs=placed, out_specs=P("ch", "ctx"), check_vma=False
    )
```

```python
import jax
import jax.numpy as jnp
from jax import lax
from jax.experimental import pallas as pl
from jax.experimental.pallas import tpu as pltpu
from jax.sharding import PartitionSpec as P

SEGMENTS = 8
LANES = 128
ORDER = 16
ROW = 8
SCOPED = 16 * 2**20
F32 = jnp.float32
BF16 = jnp.bfloat16
NT = (((1,), (1,)), ((), ()))
TN = (((0,), (0,)), ((), ()))

FOUR, PAIR = 4, 7
DECAY, FADE, WEIGHT, GROWTH = 0, 1, 4, 5
ALL, ALL_SEAM, AHEAD, AHEAD_SEAM, OVER_PAIR, OVER_Y = 7, 10, 13, 16, 18, 23
TABLES = 29
SKIP, FIRST = 9, 10
EDGES = 16


def call(kernel, name, out, scratch=(), held=True, outside=(), unread=()):
    whole = pl.BlockSpec(memory_space=pltpu.VMEM)
    if not held:
        whole = pl.BlockSpec(memory_space=pl.ANY)
    place = (lambda o: pltpu.VMEM(o.shape, o.dtype)) if held else (lambda o: o)

    def run(*args):
        spaces = [
            pl.ANY if i in unread else pltpu.HBM if i in outside else pltpu.VMEM
            for i in range(len(args))
        ]
        return pl.pallas_call(
            kernel,
            in_specs=[pl.BlockSpec(memory_space=space) for space in spaces],
            out_specs=jax.tree.map(lambda _: whole, out),
            out_shape=jax.tree.map(place, out),
            scratch_shapes=list(scratch),
            compiler_params=pltpu.CompilerParams(vmem_limit_bytes=SCOPED),
            name=name,
        )(*(pltpu.with_memory_space_constraint(a, space) for a, space in zip(args, spaces)))

    return run


def order_matrix(span):
    steps = span // SEGMENTS
    row = lax.broadcasted_iota(jnp.int32, (span, span), 0)
    col = lax.broadcasted_iota(jnp.int32, (span, span), 1)
    return jnp.where(col == (row & (SEGMENTS - 1)) * steps + (row >> 3), 1.0, 0.0).astype(BF16)


def segment_index():
    return lax.broadcasted_iota(jnp.int32, (SEGMENTS, LANES), 0)


def by_group(channels, body):
    def step(g, nothing):
        body(pl.ds(pl.multiple_of(g * LANES, LANES), LANES))
        return nothing

    lax.fori_loop(0, channels // LANES, step, 0)


def place_of():
    here = lax.axis_index("ctx")
    return here // ROW, lax.rem(here, ROW)


def tables_kernel(span, basis, modes, tables):
    y, z = place_of()
    damping, residue = modes[0], modes[1]

    def fade(by):
        return jnp.exp(-damping * by)

    def only(flag, value):
        return jnp.where(flag, value, 0.0)

    for i in range(4):
        tables[DECAY + i] = basis[i]
    tables[WEIGHT] = residue * jnp.sqrt(damping)
    tables[GROWTH] = fade(-1.0)
    tables[GROWTH + 1] = fade(-2.0)
    place = z & (FOUR - 1)
    for q in range(3):
        tables[ALL + q] = fade(float((3 - q) * span))
        tables[ALL_SEAM + q] = fade(float((3 - q) * span - 2))
        ahead = jnp.maximum(place - 1 - q, 0) * span
        tables[AHEAD + q] = only(q < place, fade(ahead.astype(F32)))
    for q in range(2):
        seen = jnp.maximum((place - 1 - q) * span - 2, 0)
        tables[AHEAD_SEAM + q] = only(q + 1 < place, fade(seen.astype(F32)))
    older = (z & FOUR) != 0
    ahead = place * span
    whole = fade(float(FOUR * span))
    tables[OVER_PAIR] = only(older, fade(ahead.astype(F32)))
    seen = jnp.maximum(ahead - 2, 0).astype(F32)
    tables[OVER_PAIR + 1] = only(older & (ahead > 0), fade(seen))
    tables[OVER_PAIR + 2] = jnp.where(older, whole, 1.0)
    tables[OVER_PAIR + 3] = jnp.where(older, 1.0, whole)
    tables[OVER_PAIR + 4] = fade(float(FOUR * span - 2))
    for s in range(3):
        ahead = (ROW * s + z) * span
        tables[OVER_Y + s] = only(y >= s + 1, fade(ahead.astype(F32)))
        seen = jnp.maximum(ahead - 2, 0).astype(F32)
        tables[OVER_Y + 3 + s] = only((y >= s + 1) & (ahead > 0), fade(seen))


def make_tables(span, basis, modes):
    out = jax.ShapeDtypeStruct((TABLES, *basis.shape[1:]), F32)
    return call(lambda *refs: tables_kernel(span, *refs), "tables", out)(basis, modes)


def states_kernel(
    key_hbm,
    value_hbm,
    query_hbm,
    taps_hbm,
    damping_hbm,
    residue_hbm,
    skip_hbm,
    message,
    gated,
    params,
    basis,
    modes,
    order,
    raw,
    tail,
    taps_in,
    skip,
    streams,
    state,
    edges,
    start_fade,
    sems,
):
    channels, span = key_hbm.shape
    steps = span // SEGMENTS
    fixed = [
        pltpu.make_async_copy(src, dst, sems.at[i])
        for i, (src, dst) in enumerate(
            (
                (damping_hbm, modes.at[0]),
                (taps_hbm, taps_in),
                (residue_hbm, modes.at[1]),
                (skip_hbm, skip),
                (query_hbm.at[:, span - LANES :], tail),
            )
        )
    ]

    big = [
        pltpu.make_async_copy(src, raw.at[s], sems.at[len(fixed) + s])
        for s, src in enumerate((key_hbm, value_hbm))
    ]
    for c in fixed[:2]:
        c.start()
    for c in big:
        c.start()
    for c in fixed[2:]:
        c.start()
    order[...] = order_matrix(span)
    segment = segment_index()
    params[...] = jnp.zeros_like(params)
    edges[...] = jnp.zeros_like(edges)
    for c in big + fixed:
        c.wait()
    for s in range(2):
        streams[s] = lax.dot_general(order[...], raw[s], NT, preferred_element_type=F32)
    basis[DECAY] = jnp.exp(-modes[0])
    for i in range(3):
        basis[FADE + i] = jnp.exp(-modes[0] * float(steps << i))
    start_fade[...] = jnp.exp(-modes[0] * float(span - 2))
    for i in range(9):
        params[i : i + 1, :] = taps_in[(1 + i // 3) % 3, i % 3, :][None, :]
    params[SKIP : SKIP + 1, :] = skip[...]
    for s in range(2):
        edges[2 * s : 2 * s + 1, :] = streams[s, 0:1, :]
        edges[2 * s + 1 : 2 * s + 2, :] = streams[s, SEGMENTS : SEGMENTS + 1, :]
        edges[4 + 2 * s : 5 + 2 * s, :] = streams[s, span - SEGMENTS - 1 : span - SEGMENTS, :]
        edges[5 + 2 * s : 6 + 2 * s, :] = streams[s, span - 1 : span, :]
    row = lax.broadcasted_iota(jnp.int32, (8, LANES), 0)
    col = lax.broadcasted_iota(jnp.int32, (8, LANES), 1)
    pick = jnp.where(col == LANES - 2 + row, 1.0, 0.0).astype(BF16)
    edges[8:16, :] = lax.dot_general(pick, tail[...], NT, preferred_element_type=F32)
    message[EDGES:, :] = edges[...].astype(BF16)

    def group(lanes):
        taps = [params[i : i + 1, lanes] for i in range(6)]
        decay = [basis[DECAY, r : r + 1, lanes] for r in range(ORDER)]

        def at(s, a):
            if a >= 0:
                return streams[s, a * SEGMENTS : (a + 1) * SEGMENTS, lanes]
            rolled = pltpu.roll(at(s, a + steps), 1, 0)
            return jnp.where(segment == 0, 0.0, rolled)

        held = [jnp.zeros((SEGMENTS, LANES), F32) for _ in range(ORDER)]
        for a in range(steps):
            f = [
                taps[3 * s] * at(s, a)
                + taps[3 * s + 1] * at(s, a - 1)
                + taps[3 * s + 2] * at(s, a - 2)
                for s in range(2)
            ]
            u = f[0] * f[1]
            if a < 2:
                params[FIRST + a : FIRST + a + 1, lanes] = f[0][0:1]
                params[FIRST + 2 + a : FIRST + 3 + a, lanes] = f[1][0:1]
                u = jnp.where(segment == 0, 0.0, u)
            gated[a * SEGMENTS : (a + 1) * SEGMENTS, lanes] = u
            for r in range(ORDER):
                held[r] = held[r] * decay[r] + u
        for r in range(ORDER):
            total = held[r]
            for i in range(3):
                fade = basis[FADE + i, r : r + 1, lanes]
                total = total + fade * pltpu.roll(total, 1 << i, 0)
            state[r : r + 1, lanes] = total[SEGMENTS - 1 :]

    by_group(channels, group)
    at = lambda i: params[FIRST + i : FIRST + i + 1, :]
    start = start_fade[...] * (basis[DECAY] * (at(0) * at(2)) + at(1) * at(3))
    total = state[...] + jnp.where(lax.axis_index("ctx") == 0, start, 0.0)
    message[0:ORDER, :] = total.astype(BF16)


def states(key_in, value_in, query_in, taps, damping, residue, skip):
    channels, span = key_in.shape
    shape = jax.ShapeDtypeStruct
    out = [
        shape((EDGES + 16, channels), BF16),
        shape((span, channels), F32),
        shape((16, channels), F32),
        shape((4, ORDER, channels), F32),
        shape((2, ORDER, channels), F32),
        shape((span, span), BF16),
    ]
    scratch = [
        pltpu.VMEM((2, channels, span), BF16),
        pltpu.VMEM((channels, LANES), BF16),
        pltpu.VMEM(taps.shape, F32),
        pltpu.VMEM(skip.shape, F32),
        pltpu.VMEM((2, span, channels), F32),
        pltpu.VMEM((ORDER, channels), F32),
        pltpu.VMEM((16, channels), F32),
        pltpu.VMEM((ORDER, channels), F32),
        pltpu.SemaphoreType.DMA((7,)),
    ]
    return call(states_kernel, "states", out, scratch, outside=range(7))(
        key_in, value_in, query_in, taps, damping, residue, skip
    )


def local_kernel(
    gated,
    query_hbm,
    params,
    tables,
    order,
    after,
    local,
    gate,
    carry,
    reach,
    raw,
    stream,
    sem,
):
    channels, span = query_hbm.shape
    steps = span // SEGMENTS
    copy = pltpu.make_async_copy(query_hbm, raw, sem)
    copy.start()
    copy.wait()
    stream[...] = lax.dot_general(order[...], raw[...], NT, preferred_element_type=F32)
    segment = segment_index()

    def group(lanes):
        taps = [params[6 + i : 7 + i, lanes] for i in range(3)]
        skip = params[SKIP : SKIP + 1, lanes]
        decay = [tables[DECAY, r : r + 1, lanes] for r in range(ORDER)]
        weight = [tables[WEIGHT, r : r + 1, lanes] for r in range(ORDER)]

        def at(a):
            if a >= 0:
                return stream[a * SEGMENTS : (a + 1) * SEGMENTS, lanes]
            rolled = pltpu.roll(at(a + steps), 1, 0)
            return jnp.where(segment == 0, 0.0, rolled)

        held = [jnp.zeros((SEGMENTS, LANES), F32) for _ in range(ORDER)]
        for a in range(steps):
            here = slice(a * SEGMENTS, (a + 1) * SEGMENTS)
            u = gated[here, lanes]
            parts = [skip * u, None, None, None]
            for r in range(ORDER):
                held[r] = held[r] * decay[r] + u
                term = weight[r] * held[r]
                parts[r % 4] = term if parts[r % 4] is None else parts[r % 4] + term
            local[here, lanes] = (parts[0] + parts[1]) + (parts[2] + parts[3])
            gate[here, lanes] = taps[0] * at(a) + taps[1] * at(a - 1) + taps[2] * at(a - 2)
        for r in range(ORDER):
            total = held[r]
            far = jnp.ones((SEGMENTS, LANES), F32)
            for i in range(3):
                fade = tables[FADE + i, r : r + 1, lanes]
                by = 1 << i
                total = total + jnp.where(segment < by, 0.0, fade * pltpu.roll(total, by, 0))
                far = jnp.where((segment & by) != 0, far * fade, far)
            total = jnp.where(segment < 1, 0.0, pltpu.roll(total, 1, 0))
            here = slice(r * SEGMENTS, (r + 1) * SEGMENTS)
            scale = weight[r] * decay[r]
            carry[here, lanes] = scale * total
            reach[here, lanes] = scale * far

    by_group(channels, group)


def local_scan(gated, query_in, params, tables, order, after):
    channels, span = query_in.shape
    shape = jax.ShapeDtypeStruct
    out = [
        shape((span, channels), F32),
        shape((span, channels), F32),
        shape((ORDER * SEGMENTS, channels), F32),
        shape((ORDER * SEGMENTS, channels), F32),
    ]
    scratch = [
        pltpu.VMEM((channels, span), BF16),
        pltpu.VMEM((span, channels), F32),
        pltpu.SemaphoreType.DMA,
    ]
    return call(local_kernel, "local_scan", out, scratch, outside=(1,), unread=(5,))(
        gated, query_in, params, tables, order, after
    )


def unpack(message):
    return message[0:ORDER, :].astype(F32), message[EDGES:, :].astype(F32)


def gated_start(params, new, old):
    out = []
    for s in range(2):
        near, mid, far = (params[3 * s + i : 3 * s + i + 1, :] for i in range(3))
        first, second = new[2 * s : 2 * s + 1], new[2 * s + 1 : 2 * s + 2]
        before, last = old[4 + 2 * s : 5 + 2 * s], old[5 + 2 * s : 6 + 2 * s]
        out.append(
            (near * first + mid * last + far * before, near * second + mid * first + far * last)
        )
    (k0, k1), (v0, v1) = out
    return k0 * v0, k1 * v1


def in_order(place, mine, swapped):
    one, two, three = swapped
    pick = lambda q, m, a, b, c: jnp.where(
        place == q, m, jnp.where((place ^ 1) == q, a, jnp.where((place ^ 2) == q, b, c))
    )
    return [
        tuple(pick(q, m, a, b, c) for m, a, b, c in zip(mine, one, two, three)) for q in range(4)
    ]


def send(message, state, first, last):
    message[0:ORDER, :] = state.astype(BF16)
    row = lax.broadcasted_iota(jnp.int32, first.shape, 0)
    message[EDGES:, :] = jnp.where(row < 4, first, last).astype(BF16)


def merge_four_kernel(mine, three, two, one, params, tables, message, before, border):
    _, z = place_of()
    place = z & (FOUR - 1)
    blocks = in_order(place, unpack(mine), [unpack(m) for m in (one, two, three)])
    total, ahead = blocks[3][0], jnp.zeros_like(before)
    for q in range(3):
        total = total + tables[ALL + q] * blocks[q][0]
        ahead = ahead + tables[AHEAD + q] * blocks[q][0]
        u0, u1 = gated_start(params, blocks[q + 1][1], blocks[q][1])
        seam = tables[DECAY] * u0 + u1
        total = total + tables[ALL_SEAM + q] * seam
        if q < 2:
            ahead = ahead + tables[AHEAD_SEAM + q] * seam
    send(message, total, blocks[0][1], blocks[3][1])
    before[...] = ahead
    last = jnp.zeros_like(border)
    for q in range(3):
        last = jnp.where(place == q + 1, blocks[q][1], last)
    border[...] = last


def merge_four(mine, swapped, params, tables):
    channels = mine.shape[1]
    shape = jax.ShapeDtypeStruct
    out = [shape(mine.shape, BF16), shape((ORDER, channels), F32), shape((16, channels), F32)]
    return call(merge_four_kernel, "merge_four", out)(mine, *swapped, params, tables)


def merge_pair_kernel(
    mine, theirs, before, border, params, tables, after, message, before_out, border_out
):
    at = OVER_PAIR
    _, z = place_of()
    older = (z & FOUR) != 0
    first = (z & (FOUR - 1)) == 0
    my_state, my_edges = unpack(mine)
    state, edges = unpack(theirs)
    new = jnp.where(older, my_edges, edges)
    old = jnp.where(older, edges, my_edges)
    u0, u1 = gated_start(params, new, old)
    seam = tables[DECAY] * u0 + u1
    total = tables[at + 2] * state + tables[at + 3] * my_state + tables[at + 4] * seam
    send(message, total, old, new)
    before_out[...] = before[...] + tables[at] * state + tables[at + 1] * seam
    border_out[...] = jnp.where(older & first, edges, border[...])


def merge_pair(mine, theirs, before, border, params, tables, after):
    shape = jax.ShapeDtypeStruct
    out = [shape(mine.shape, BF16), shape(before.shape, F32), shape(border.shape, F32)]
    return call(merge_pair_kernel, "merge_pair", out, unread=(6,))(
        mine, theirs, before, border, params, tables, after
    )


def gate_kernel(
    mine,
    row2,
    row3,
    row1,
    before_in,
    border_in,
    local,
    gate,
    carry,
    reach,
    params,
    tables,
    out,
    before,
    starts,
):
    span, channels = local.shape
    steps = span // SEGMENTS
    y, z = place_of()
    lying = in_order(y, unpack(mine), [unpack(m) for m in (row1, row2, row3)])
    rows = [unpack(mine)]
    for s in range(1, 4):
        pick = lambda a, b, c: jnp.where(y - s == 0, a, jnp.where(y - s == 1, b, c))
        rows.append(tuple(pick(a, b, c) for a, b, c in zip(*lying[:3])))
    total = before_in[...]
    for s in range(3):
        u0, u1 = gated_start(params, rows[s][1], rows[s + 1][1])
        total = total + tables[OVER_Y + s] * rows[s + 1][0]
        total = total + tables[OVER_Y + 3 + s] * (tables[DECAY] * u0 + u1)
    border = jnp.where((z == 0) & (y >= 1), rows[1][1], border_in[...])
    u = [None, None]
    p = lambda i: params[i : i + 1, :]
    e = lambda i: border[4 + i : 5 + i]
    u[0] = (p(FIRST) + p(1) * e(1) + p(2) * e(0)) * (p(FIRST + 2) + p(4) * e(3) + p(5) * e(2))
    u[1] = (p(FIRST + 1) + p(2) * e(1)) * (p(FIRST + 3) + p(5) * e(3))
    before[...] = total + tables[GROWTH] * u[0] + tables[GROWTH + 1] * u[1]
    grown = jnp.sum(tables[WEIGHT] * tables[GROWTH], axis=0, keepdims=True)
    starts[0:1, :] = p(SKIP) * u[0] - grown * u[1]
    starts[1:2, :] = p(SKIP) * u[1]
    starts[2:3, :] = p(7) * e(5) + p(8) * e(4)
    starts[3:4, :] = p(8) * e(5)
    segment = segment_index()

    def group(lanes):
        decay, term = [], []
        for r in range(ORDER):
            here = slice(r * SEGMENTS, (r + 1) * SEGMENTS)
            term.append(carry[here, lanes] + reach[here, lanes] * before[r : r + 1, lanes])
            decay.append(tables[DECAY, r : r + 1, lanes])
        for pair in range(steps // 2):
            both = []
            for a in (2 * pair, 2 * pair + 1):
                here = slice(a * SEGMENTS, (a + 1) * SEGMENTS)
                parts = [local[here, lanes], None, None, None]
                times = gate[here, lanes]
                if a < 2:
                    first = segment == 0
                    parts[0] = parts[0] + jnp.where(first, starts[a : a + 1, lanes], 0.0)
                    times = times + jnp.where(first, starts[2 + a : 3 + a, lanes], 0.0)
                for r in range(ORDER):
                    parts[r % 4] = term[r] if parts[r % 4] is None else parts[r % 4] + term[r]
                    term[r] = term[r] * decay[r]
                both.append(((parts[0] + parts[1]) + (parts[2] + parts[3])) * times)
            here = slice(pair * 2 * SEGMENTS, (pair + 1) * 2 * SEGMENTS)
            out[here, lanes] = jnp.concatenate(both, axis=0).astype(BF16)

    by_group(channels, group)


def gate_all(messages, before, border, local, gate, carry, reach, params, tables):
    out = jax.ShapeDtypeStruct(local.shape, BF16)
    scratch = [pltpu.VMEM(before.shape, F32), pltpu.VMEM((8, before.shape[1]), F32)]
    return call(gate_kernel, "gated", out, scratch)(
        *messages, before, border, local, gate, carry, reach, params, tables
    )


def blocks_kernel(weight_hbm, after, out, sems):
    columns = out.shape[1] // sems.shape[0]
    me = lax.axis_index("ch")
    copies = []
    for k in range(sems.shape[0]):
        at = pl.ds(pl.multiple_of((me ^ (2 * k)) * columns, columns), columns)
        copies.append(
            pltpu.make_async_copy(
                weight_hbm.at[:, at], out.at[:, k * columns : (k + 1) * columns], sems.at[k]
            )
        )
    for c in copies:
        c.start()
    for c in copies:
        c.wait()


def weight_blocks(weight, after):
    channels, width = weight.shape
    chips = lax.axis_size("ch") // 2
    out = jax.ShapeDtypeStruct((channels, width // 2), BF16)
    scratch = [pltpu.SemaphoreType.DMA((chips,))]
    return call(blocks_kernel, "weight_blocks", out, scratch, outside=(0,), unread=(1,))(weight, after)


def near_kernel(mine, weight, out):
    out[...] = jnp.dot(mine[...], weight[...], preferred_element_type=F32)


def near_sums(mine, weight):
    out = jax.ShapeDtypeStruct((mine.shape[0], weight.shape[1]), F32)
    return call(near_kernel, "near_sums", out)(mine, weight)


def project(near, other, far, name, wanted, dtype):
    span = near.shape[0]
    half = span // 2
    columns = far.shape[1] // lax.axis_size("ch")

    def kernel(near_ref, other_ref, far_ref, *out_refs):
        for out_ref, parts in zip(out_refs, wanted):
            for i, (k, part) in enumerate(parts):
                block = lax.axis_index("ch") ^ (2 * k)
                there = pl.ds(pl.multiple_of(block * columns, columns), columns)
                rows = slice(part * half, (part + 1) * half)
                total = near_ref[rows, k * columns : (k + 1) * columns] + jnp.dot(
                    other_ref[rows, :], far_ref[:, there], preferred_element_type=F32
                )
                out_ref[i * half : (i + 1) * half, :] = total.astype(dtype)

    out = [jax.ShapeDtypeStruct((half * len(parts), columns), dtype) for parts in wanted]
    return call(kernel, name, out)(near, other, far)


def relay_kernel(passing, own, out):
    out[...] = (passing[...].astype(F32) + own[...]).astype(BF16)


def relay(passing, own):
    return call(relay_kernel, "relay", jax.ShapeDtypeStruct(own.shape, BF16))(passing, own)


def finish_kernel(own, direct1, direct3, joined1, joined3, order, out, result, sems):
    half = joined1.shape[0]
    columns = own.shape[1]
    copies = []
    for i in range(2):
        here = slice(i * columns // 2, (i + 1) * columns // 2)
        top = own[0:half, here] + (direct1[:, here].astype(F32) + joined3[:, here].astype(F32))
        low = own[half:, here] + (direct3[:, here].astype(F32) + joined1[:, here].astype(F32))
        total = jnp.concatenate([top.astype(BF16), low.astype(BF16)], axis=0)
        result[here, :] = lax.dot_general(
            total, order[...], TN, preferred_element_type=F32
        ).astype(BF16)
        copies.append(pltpu.make_async_copy(result.at[here, :], out.at[here, :], sems.at[i]))
        copies[-1].start()
    for c in copies:
        c.wait()


def finish(own, *received):
    span, columns = own.shape
    out = jax.ShapeDtypeStruct((columns, span), BF16)
    scratch = [pltpu.VMEM(out.shape, BF16), pltpu.SemaphoreType.DMA((2,))]
    return call(finish_kernel, "finish", out, scratch, held=False)(own, *received)


def per_device(
    query_in, key_in, value_in, short_taps, modal_residue, mode_damping_speed, skip_gain, out_weight
):
    channels = query_in.shape[0]
    n_ctx, n_ch = lax.axis_size("ctx"), lax.axis_size("ch")
    sibling = [(i, i ^ 1) for i in range(n_ch)]
    message, gated, params, basis, modes, order = states(
        key_in,
        value_in,
        query_in,
        jnp.transpose(short_taps, (0, 2, 1)),
        mode_damping_speed.T,
        modal_residue.T,
        skip_gain[None, :],
    )
    def across(value, by):
        return lax.ppermute(value, "ctx", [(i, i ^ by) for i in range(n_ctx)])

    swapped = [across(message, k) for k in (3, 2, 1)]
    tables = make_tables(query_in.shape[1], basis, modes)
    message, before, border = merge_four(message, swapped, params, tables)
    later, _ = lax.optimization_barrier((out_weight, message))
    far = lax.ppermute(later, "ch", sibling)
    theirs = across(message, PAIR)
    weight = weight_blocks(out_weight, message)
    message, before, border = merge_pair(message, theirs, before, border, params, tables, weight)
    local, gate, carry, reach = local_scan(gated, query_in, params, tables, order, message)
    messages = [message] + [across(message, k * ROW) for k in (2, 3, 1)]

    own = gate_all(messages, before, border, local, gate, carry, reach, params, tables)
    other = lax.ppermute(own, "ch", sibling)

    def swap(value, k):
        return lax.ppermute(value, "ch", [(i, i ^ (2 * k)) for i in range(n_ch)])

    operands = (near_sums(own, weight), other, far)
    over3, over1 = project(*operands, "opposite", [[(2, 1)], [(2, 0)]], BF16)
    over3, over1 = swap(over3, 3), swap(over1, 1)
    direct3, direct1 = project(*operands, "neighbours", [[(3, 1)], [(1, 0)]], BF16)
    direct3, direct1 = swap(direct3, 3), swap(direct1, 1)
    mine3, mine1 = project(*operands, "joining", [[(3, 0)], [(1, 1)]], F32)
    (kept,) = project(*operands, "kept", [[(0, 0), (0, 1)]], F32)
    joined1 = swap(relay(over3, mine1), 1)
    joined3 = swap(relay(over1, mine3), 3)
    return finish(kept, direct1, direct3, joined1, joined3, order)


def solution(mesh):
    placed = (
        P("ch", "ctx"),
        P("ch", "ctx"),
        P("ch", "ctx"),
        P(None, "ch", None),
        P("ch", None),
        P("ch", None),
        P("ch"),
        P("ch", None),
    )
    return jax.shard_map(
        per_device, mesh=mesh, in_specs=placed, out_specs=P("ch", "ctx"), check_vma=False
    )
```

```python
import jax
import jax.numpy as jnp
from jax import lax
from jax.experimental import pallas as pl
from jax.experimental.pallas import tpu as pltpu
from jax.sharding import PartitionSpec as P

SEGMENTS = 8
LANES = 128
ORDER = 16
ROW = 8
SCOPED = 16 * 2**20
F32 = jnp.float32
BF16 = jnp.bfloat16
NT = (((1,), (1,)), ((), ()))
TN = (((0,), (0,)), ((), ()))

FOUR, PAIR = 4, 7
DECAY, FADE, WEIGHT, GROWTH = 0, 1, 4, 5
ALL, ALL_SEAM, AHEAD, AHEAD_SEAM, OVER_PAIR, OVER_Y = 7, 10, 13, 16, 18, 23
TABLES = 29
SKIP, FIRST = 9, 10
EDGES = 16


def call(kernel, name, out, scratch=(), held=True, outside=(), unread=()):
    whole = pl.BlockSpec(memory_space=pltpu.VMEM)
    if not held:
        whole = pl.BlockSpec(memory_space=pl.ANY)
    place = (lambda o: pltpu.VMEM(o.shape, o.dtype)) if held else (lambda o: o)

    def run(*args):
        spaces = [
            pl.ANY if i in unread else pltpu.HBM if i in outside else pltpu.VMEM
            for i in range(len(args))
        ]
        return pl.pallas_call(
            kernel,
            in_specs=[pl.BlockSpec(memory_space=space) for space in spaces],
            out_specs=jax.tree.map(lambda _: whole, out),
            out_shape=jax.tree.map(place, out),
            scratch_shapes=list(scratch),
            compiler_params=pltpu.CompilerParams(vmem_limit_bytes=SCOPED),
            name=name,
        )(*(pltpu.with_memory_space_constraint(a, space) for a, space in zip(args, spaces)))

    return run


def order_matrix(span):
    steps = span // SEGMENTS
    row = lax.broadcasted_iota(jnp.int32, (span, span), 0)
    col = lax.broadcasted_iota(jnp.int32, (span, span), 1)
    return jnp.where(col == (row & (SEGMENTS - 1)) * steps + (row >> 3), 1.0, 0.0).astype(BF16)


def segment_index():
    return lax.broadcasted_iota(jnp.int32, (SEGMENTS, LANES), 0)


def by_group(channels, body):
    def step(g, nothing):
        body(pl.ds(pl.multiple_of(g * LANES, LANES), LANES))
        return nothing

    lax.fori_loop(0, channels // LANES, step, 0)


def place_of():
    here = lax.axis_index("ctx")
    return here // ROW, lax.rem(here, ROW)


def tables_kernel(span, basis, modes, tables):
    y, z = place_of()
    damping, residue = modes[0], modes[1]

    def fade(by):
        return jnp.exp(-damping * by)

    def only(flag, value):
        return jnp.where(flag, value, 0.0)

    for i in range(4):
        tables[DECAY + i] = basis[i]
    tables[WEIGHT] = residue * jnp.sqrt(damping)
    tables[GROWTH] = fade(-1.0)
    tables[GROWTH + 1] = fade(-2.0)
    place = z & (FOUR - 1)
    for q in range(3):
        tables[ALL + q] = fade(float((3 - q) * span))
        tables[ALL_SEAM + q] = fade(float((3 - q) * span - 2))
        ahead = jnp.maximum(place - 1 - q, 0) * span
        tables[AHEAD + q] = only(q < place, fade(ahead.astype(F32)))
    for q in range(2):
        seen = jnp.maximum((place - 1 - q) * span - 2, 0)
        tables[AHEAD_SEAM + q] = only(q + 1 < place, fade(seen.astype(F32)))
    older = (z & FOUR) != 0
    ahead = place * span
    whole = fade(float(FOUR * span))
    tables[OVER_PAIR] = only(older, fade(ahead.astype(F32)))
    seen = jnp.maximum(ahead - 2, 0).astype(F32)
    tables[OVER_PAIR + 1] = only(older & (ahead > 0), fade(seen))
    tables[OVER_PAIR + 2] = jnp.where(older, whole, 1.0)
    tables[OVER_PAIR + 3] = jnp.where(older, 1.0, whole)
    tables[OVER_PAIR + 4] = fade(float(FOUR * span - 2))
    for s in range(3):
        ahead = (ROW * s + z) * span
        tables[OVER_Y + s] = only(y >= s + 1, fade(ahead.astype(F32)))
        seen = jnp.maximum(ahead - 2, 0).astype(F32)
        tables[OVER_Y + 3 + s] = only((y >= s + 1) & (ahead > 0), fade(seen))


def make_tables(span, basis, modes):
    out = jax.ShapeDtypeStruct((TABLES, *basis.shape[1:]), F32)
    return call(lambda *refs: tables_kernel(span, *refs), "tables", out)(basis, modes)


def states_kernel(
    key_hbm,
    value_hbm,
    query_hbm,
    taps_hbm,
    damping_hbm,
    residue_hbm,
    skip_hbm,
    message,
    gated,
    params,
    basis,
    modes,
    order,
    raw,
    tail,
    taps_in,
    skip,
    streams,
    state,
    edges,
    start_fade,
    sems,
):
    channels, span = key_hbm.shape
    steps = span // SEGMENTS
    fixed = [
        pltpu.make_async_copy(src, dst, sems.at[i])
        for i, (src, dst) in enumerate(
            (
                (damping_hbm, modes.at[0]),
                (taps_hbm, taps_in),
                (residue_hbm, modes.at[1]),
                (skip_hbm, skip),
                (query_hbm.at[:, span - LANES :], tail),
            )
        )
    ]

    big = [
        pltpu.make_async_copy(src, raw.at[s], sems.at[len(fixed) + s])
        for s, src in enumerate((key_hbm, value_hbm))
    ]
    for c in fixed[:2]:
        c.start()
    for c in big:
        c.start()
    for c in fixed[2:]:
        c.start()
    order[...] = order_matrix(span)
    segment = segment_index()
    params[...] = jnp.zeros_like(params)
    edges[...] = jnp.zeros_like(edges)
    for c in big + fixed:
        c.wait()
    for s in range(2):
        streams[s] = lax.dot_general(order[...], raw[s], NT, preferred_element_type=F32)
    basis[DECAY] = jnp.exp(-modes[0])
    for i in range(3):
        basis[FADE + i] = jnp.exp(-modes[0] * float(steps << i))
    start_fade[...] = jnp.exp(-modes[0] * float(span - 2))
    for i in range(9):
        params[i : i + 1, :] = taps_in[(1 + i // 3) % 3, i % 3, :][None, :]
    params[SKIP : SKIP + 1, :] = skip[...]
    for s in range(2):
        edges[2 * s : 2 * s + 1, :] = streams[s, 0:1, :]
        edges[2 * s + 1 : 2 * s + 2, :] = streams[s, SEGMENTS : SEGMENTS + 1, :]
        edges[4 + 2 * s : 5 + 2 * s, :] = streams[s, span - SEGMENTS - 1 : span - SEGMENTS, :]
        edges[5 + 2 * s : 6 + 2 * s, :] = streams[s, span - 1 : span, :]
    row = lax.broadcasted_iota(jnp.int32, (8, LANES), 0)
    col = lax.broadcasted_iota(jnp.int32, (8, LANES), 1)
    pick = jnp.where(col == LANES - 2 + row, 1.0, 0.0).astype(BF16)
    edges[8:16, :] = lax.dot_general(pick, tail[...], NT, preferred_element_type=F32)
    message[EDGES:, :] = edges[...].astype(BF16)

    def group(lanes):
        taps = [params[i : i + 1, lanes] for i in range(6)]
        decay = [basis[DECAY, r : r + 1, lanes] for r in range(ORDER)]

        def at(s, a):
            if a >= 0:
                return streams[s, a * SEGMENTS : (a + 1) * SEGMENTS, lanes]
            rolled = pltpu.roll(at(s, a + steps), 1, 0)
            return jnp.where(segment == 0, 0.0, rolled)

        held = [jnp.zeros((SEGMENTS, LANES), F32) for _ in range(ORDER)]
        for a in range(steps):
            f = [
                taps[3 * s] * at(s, a)
                + taps[3 * s + 1] * at(s, a - 1)
                + taps[3 * s + 2] * at(s, a - 2)
                for s in range(2)
            ]
            u = f[0] * f[1]
            if a < 2:
                params[FIRST + a : FIRST + a + 1, lanes] = f[0][0:1]
                params[FIRST + 2 + a : FIRST + 3 + a, lanes] = f[1][0:1]
                u = jnp.where(segment == 0, 0.0, u)
            gated[a * SEGMENTS : (a + 1) * SEGMENTS, lanes] = u
            for r in range(ORDER):
                held[r] = held[r] * decay[r] + u
        for r in range(ORDER):
            total = held[r]
            for i in range(3):
                fade = basis[FADE + i, r : r + 1, lanes]
                total = total + fade * pltpu.roll(total, 1 << i, 0)
            state[r : r + 1, lanes] = total[SEGMENTS - 1 :]

    by_group(channels, group)
    at = lambda i: params[FIRST + i : FIRST + i + 1, :]
    start = start_fade[...] * (basis[DECAY] * (at(0) * at(2)) + at(1) * at(3))
    total = state[...] + jnp.where(lax.axis_index("ctx") == 0, start, 0.0)
    message[0:ORDER, :] = total.astype(BF16)


def states(key_in, value_in, query_in, taps, damping, residue, skip):
    channels, span = key_in.shape
    shape = jax.ShapeDtypeStruct
    out = [
        shape((EDGES + 16, channels), BF16),
        shape((span, channels), F32),
        shape((16, channels), F32),
        shape((4, ORDER, channels), F32),
        shape((2, ORDER, channels), F32),
        shape((span, span), BF16),
    ]
    scratch = [
        pltpu.VMEM((2, channels, span), BF16),
        pltpu.VMEM((channels, LANES), BF16),
        pltpu.VMEM(taps.shape, F32),
        pltpu.VMEM(skip.shape, F32),
        pltpu.VMEM((2, span, channels), F32),
        pltpu.VMEM((ORDER, channels), F32),
        pltpu.VMEM((16, channels), F32),
        pltpu.VMEM((ORDER, channels), F32),
        pltpu.SemaphoreType.DMA((7,)),
    ]
    return call(states_kernel, "states", out, scratch, outside=range(7))(
        key_in, value_in, query_in, taps, damping, residue, skip
    )


def local_kernel(
    gated,
    query_hbm,
    params,
    tables,
    order,
    after,
    local,
    gate,
    carry,
    reach,
    raw,
    stream,
    sem,
):
    channels, span = query_hbm.shape
    steps = span // SEGMENTS
    copy = pltpu.make_async_copy(query_hbm, raw, sem)
    copy.start()
    copy.wait()
    stream[...] = lax.dot_general(order[...], raw[...], NT, preferred_element_type=F32)
    segment = segment_index()

    def group(lanes):
        taps = [params[6 + i : 7 + i, lanes] for i in range(3)]
        skip = params[SKIP : SKIP + 1, lanes]
        decay = [tables[DECAY, r : r + 1, lanes] for r in range(ORDER)]
        weight = [tables[WEIGHT, r : r + 1, lanes] for r in range(ORDER)]

        def at(a):
            if a >= 0:
                return stream[a * SEGMENTS : (a + 1) * SEGMENTS, lanes]
            rolled = pltpu.roll(at(a + steps), 1, 0)
            return jnp.where(segment == 0, 0.0, rolled)

        held = [jnp.zeros((SEGMENTS, LANES), F32) for _ in range(ORDER)]
        for a in range(steps):
            here = slice(a * SEGMENTS, (a + 1) * SEGMENTS)
            u = gated[here, lanes]
            parts = [skip * u, None, None, None]
            for r in range(ORDER):
                held[r] = held[r] * decay[r] + u
                term = weight[r] * held[r]
                parts[r % 4] = term if parts[r % 4] is None else parts[r % 4] + term
            local[here, lanes] = (parts[0] + parts[1]) + (parts[2] + parts[3])
            gate[here, lanes] = taps[0] * at(a) + taps[1] * at(a - 1) + taps[2] * at(a - 2)
        for r in range(ORDER):
            total = held[r]
            far = jnp.ones((SEGMENTS, LANES), F32)
            for i in range(3):
                fade = tables[FADE + i, r : r + 1, lanes]
                by = 1 << i
                total = total + jnp.where(segment < by, 0.0, fade * pltpu.roll(total, by, 0))
                far = jnp.where((segment & by) != 0, far * fade, far)
            total = jnp.where(segment < 1, 0.0, pltpu.roll(total, 1, 0))
            here = slice(r * SEGMENTS, (r + 1) * SEGMENTS)
            scale = weight[r] * decay[r]
            carry[here, lanes] = scale * total
            reach[here, lanes] = scale * far

    by_group(channels, group)


def local_scan(gated, query_in, params, tables, order, after):
    channels, span = query_in.shape
    shape = jax.ShapeDtypeStruct
    out = [
        shape((span, channels), F32),
        shape((span, channels), F32),
        shape((ORDER * SEGMENTS, channels), F32),
        shape((ORDER * SEGMENTS, channels), F32),
    ]
    scratch = [
        pltpu.VMEM((channels, span), BF16),
        pltpu.VMEM((span, channels), F32),
        pltpu.SemaphoreType.DMA,
    ]
    return call(local_kernel, "local_scan", out, scratch, outside=(1,), unread=(5,))(
        gated, query_in, params, tables, order, after
    )


def unpack(message):
    return message[0:ORDER, :].astype(F32), message[EDGES:, :].astype(F32)


def gated_start(params, new, old):
    out = []
    for s in range(2):
        near, mid, far = (params[3 * s + i : 3 * s + i + 1, :] for i in range(3))
        first, second = new[2 * s : 2 * s + 1], new[2 * s + 1 : 2 * s + 2]
        before, last = old[4 + 2 * s : 5 + 2 * s], old[5 + 2 * s : 6 + 2 * s]
        out.append(
            (near * first + mid * last + far * before, near * second + mid * first + far * last)
        )
    (k0, k1), (v0, v1) = out
    return k0 * v0, k1 * v1


def in_order(place, mine, swapped):
    one, two, three = swapped
    pick = lambda q, m, a, b, c: jnp.where(
        place == q, m, jnp.where((place ^ 1) == q, a, jnp.where((place ^ 2) == q, b, c))
    )
    return [
        tuple(pick(q, m, a, b, c) for m, a, b, c in zip(mine, one, two, three)) for q in range(4)
    ]


def send(message, state, first, last):
    message[0:ORDER, :] = state.astype(BF16)
    row = lax.broadcasted_iota(jnp.int32, first.shape, 0)
    message[EDGES:, :] = jnp.where(row < 4, first, last).astype(BF16)


def merge_four_kernel(mine, three, two, one, params, tables, message, before, border):
    _, z = place_of()
    place = z & (FOUR - 1)
    blocks = in_order(place, unpack(mine), [unpack(m) for m in (one, two, three)])
    total, ahead = blocks[3][0], jnp.zeros_like(before)
    for q in range(3):
        total = total + tables[ALL + q] * blocks[q][0]
        ahead = ahead + tables[AHEAD + q] * blocks[q][0]
        u0, u1 = gated_start(params, blocks[q + 1][1], blocks[q][1])
        seam = tables[DECAY] * u0 + u1
        total = total + tables[ALL_SEAM + q] * seam
        if q < 2:
            ahead = ahead + tables[AHEAD_SEAM + q] * seam
    send(message, total, blocks[0][1], blocks[3][1])
    before[...] = ahead
    last = jnp.zeros_like(border)
    for q in range(3):
        last = jnp.where(place == q + 1, blocks[q][1], last)
    border[...] = last


def merge_four(mine, swapped, params, tables):
    channels = mine.shape[1]
    shape = jax.ShapeDtypeStruct
    out = [shape(mine.shape, BF16), shape((ORDER, channels), F32), shape((16, channels), F32)]
    return call(merge_four_kernel, "merge_four", out)(mine, *swapped, params, tables)


def merge_pair_kernel(
    mine, theirs, before, border, params, tables, after, message, before_out, border_out
):
    at = OVER_PAIR
    _, z = place_of()
    older = (z & FOUR) != 0
    first = (z & (FOUR - 1)) == 0
    my_state, my_edges = unpack(mine)
    state, edges = unpack(theirs)
    new = jnp.where(older, my_edges, edges)
    old = jnp.where(older, edges, my_edges)
    u0, u1 = gated_start(params, new, old)
    seam = tables[DECAY] * u0 + u1
    total = tables[at + 2] * state + tables[at + 3] * my_state + tables[at + 4] * seam
    send(message, total, old, new)
    before_out[...] = before[...] + tables[at] * state + tables[at + 1] * seam
    border_out[...] = jnp.where(older & first, edges, border[...])


def merge_pair(mine, theirs, before, border, params, tables, after):
    shape = jax.ShapeDtypeStruct
    out = [shape(mine.shape, BF16), shape(before.shape, F32), shape(border.shape, F32)]
    return call(merge_pair_kernel, "merge_pair", out, unread=(6,))(
        mine, theirs, before, border, params, tables, after
    )


def gate_kernel(
    mine,
    row2,
    row3,
    row1,
    before_in,
    border_in,
    local,
    gate,
    carry,
    reach,
    params,
    tables,
    out,
    before,
    starts,
):
    span, channels = local.shape
    steps = span // SEGMENTS
    y, z = place_of()
    lying = in_order(y, unpack(mine), [unpack(m) for m in (row1, row2, row3)])
    rows = [unpack(mine)]
    for s in range(1, 4):
        pick = lambda a, b, c: jnp.where(y - s == 0, a, jnp.where(y - s == 1, b, c))
        rows.append(tuple(pick(a, b, c) for a, b, c in zip(*lying[:3])))
    total = before_in[...]
    for s in range(3):
        u0, u1 = gated_start(params, rows[s][1], rows[s + 1][1])
        total = total + tables[OVER_Y + s] * rows[s + 1][0]
        total = total + tables[OVER_Y + 3 + s] * (tables[DECAY] * u0 + u1)
    border = jnp.where((z == 0) & (y >= 1), rows[1][1], border_in[...])
    u = [None, None]
    p = lambda i: params[i : i + 1, :]
    e = lambda i: border[4 + i : 5 + i]
    u[0] = (p(FIRST) + p(1) * e(1) + p(2) * e(0)) * (p(FIRST + 2) + p(4) * e(3) + p(5) * e(2))
    u[1] = (p(FIRST + 1) + p(2) * e(1)) * (p(FIRST + 3) + p(5) * e(3))
    before[...] = total + tables[GROWTH] * u[0] + tables[GROWTH + 1] * u[1]
    grown = jnp.sum(tables[WEIGHT] * tables[GROWTH], axis=0, keepdims=True)
    starts[0:1, :] = p(SKIP) * u[0] - grown * u[1]
    starts[1:2, :] = p(SKIP) * u[1]
    starts[2:3, :] = p(7) * e(5) + p(8) * e(4)
    starts[3:4, :] = p(8) * e(5)
    segment = segment_index()

    def group(lanes):
        decay, term = [], []
        for r in range(ORDER):
            here = slice(r * SEGMENTS, (r + 1) * SEGMENTS)
            term.append(carry[here, lanes] + reach[here, lanes] * before[r : r + 1, lanes])
            decay.append(tables[DECAY, r : r + 1, lanes])
        for pair in range(steps // 2):
            both = []
            for a in (2 * pair, 2 * pair + 1):
                here = slice(a * SEGMENTS, (a + 1) * SEGMENTS)
                parts = [local[here, lanes], None, None, None]
                times = gate[here, lanes]
                if a < 2:
                    first = segment == 0
                    parts[0] = parts[0] + jnp.where(first, starts[a : a + 1, lanes], 0.0)
                    times = times + jnp.where(first, starts[2 + a : 3 + a, lanes], 0.0)
                for r in range(ORDER):
                    parts[r % 4] = term[r] if parts[r % 4] is None else parts[r % 4] + term[r]
                    term[r] = term[r] * decay[r]
                both.append(((parts[0] + parts[1]) + (parts[2] + parts[3])) * times)
            here = slice(pair * 2 * SEGMENTS, (pair + 1) * 2 * SEGMENTS)
            out[here, lanes] = jnp.concatenate(both, axis=0).astype(BF16)

    by_group(channels, group)


def gate_all(messages, before, border, local, gate, carry, reach, params, tables):
    out = jax.ShapeDtypeStruct(local.shape, BF16)
    scratch = [pltpu.VMEM(before.shape, F32), pltpu.VMEM((8, before.shape[1]), F32)]
    return call(gate_kernel, "gated", out, scratch)(
        *messages, before, border, local, gate, carry, reach, params, tables
    )


def blocks_kernel(weight_hbm, after, out, sems):
    columns = out.shape[1] // sems.shape[0]
    me = lax.axis_index("ch")
    copies = []
    for k in range(sems.shape[0]):
        at = pl.ds(pl.multiple_of((me ^ (2 * k)) * columns, columns), columns)
        copies.append(
            pltpu.make_async_copy(
                weight_hbm.at[:, at], out.at[:, k * columns : (k + 1) * columns], sems.at[k]
            )
        )
    for c in copies:
        c.start()
    for c in copies:
        c.wait()


def weight_blocks(weight, after):
    channels, width = weight.shape
    chips = lax.axis_size("ch") // 2
    out = jax.ShapeDtypeStruct((channels, width // 2), BF16)
    scratch = [pltpu.SemaphoreType.DMA((chips,))]
    return call(blocks_kernel, "weight_blocks", out, scratch, outside=(0,), unread=(1,))(weight, after)


def near_kernel(mine, weight, out):
    out[...] = jnp.dot(mine[...], weight[...], preferred_element_type=F32)


def near_sums(mine, weight):
    out = jax.ShapeDtypeStruct((mine.shape[0], weight.shape[1]), F32)
    return call(near_kernel, "near_sums", out)(mine, weight)


def project(near, other, far, name, wanted, dtype):
    span = near.shape[0]
    half = span // 2
    columns = far.shape[1] // lax.axis_size("ch")

    def kernel(near_ref, other_ref, far_ref, *out_refs):
        for out_ref, parts in zip(out_refs, wanted):
            for i, (k, part) in enumerate(parts):
                block = lax.axis_index("ch") ^ (2 * k)
                there = pl.ds(pl.multiple_of(block * columns, columns), columns)
                rows = slice(part * half, (part + 1) * half)
                total = near_ref[rows, k * columns : (k + 1) * columns] + jnp.dot(
                    other_ref[rows, :], far_ref[:, there], preferred_element_type=F32
                )
                out_ref[i * half : (i + 1) * half, :] = total.astype(dtype)

    out = [jax.ShapeDtypeStruct((half * len(parts), columns), dtype) for parts in wanted]
    return call(kernel, name, out)(near, other, far)


def sides(near, other, far):
    span = near.shape[0]
    half = span // 2
    columns = far.shape[1] // lax.axis_size("ch")

    def kernel(near_ref, other_ref, far_ref, direct3, direct1, mine3, mine1):
        for k, direct, mine in ((3, direct3, mine3), (1, direct1, mine1)):
            block = lax.axis_index("ch") ^ (2 * k)
            there = pl.ds(pl.multiple_of(block * columns, columns), columns)
            total = near_ref[:, k * columns : (k + 1) * columns] + jnp.dot(
                other_ref[...], far_ref[:, there], preferred_element_type=F32
            )
            top, low = total[:half], total[half:]
            direct[...] = (low if k == 3 else top).astype(BF16)
            mine[...] = top if k == 3 else low

    out = [jax.ShapeDtypeStruct((half, columns), d) for d in (BF16, BF16, F32, F32)]
    return call(kernel, "sides", out)(near, other, far)


def relay_kernel(passing, own, out):
    out[...] = (passing[...].astype(F32) + own[...]).astype(BF16)


def relay(passing, own):
    return call(relay_kernel, "relay", jax.ShapeDtypeStruct(own.shape, BF16))(passing, own)


def finish_kernel(own, direct1, direct3, joined1, joined3, order, out, result, sems):
    half = joined1.shape[0]
    columns = own.shape[1]
    copies = []
    for i in range(2):
        here = slice(i * columns // 2, (i + 1) * columns // 2)
        top = own[0:half, here] + (direct1[:, here].astype(F32) + joined3[:, here].astype(F32))
        low = own[half:, here] + (direct3[:, here].astype(F32) + joined1[:, here].astype(F32))
        total = jnp.concatenate([top.astype(BF16), low.astype(BF16)], axis=0)
        result[here, :] = lax.dot_general(
            total, order[...], TN, preferred_element_type=F32
        ).astype(BF16)
        copies.append(pltpu.make_async_copy(result.at[here, :], out.at[here, :], sems.at[i]))
        copies[-1].start()
    for c in copies:
        c.wait()


def finish(own, *received):
    span, columns = own.shape
    out = jax.ShapeDtypeStruct((columns, span), BF16)
    scratch = [pltpu.VMEM(out.shape, BF16), pltpu.SemaphoreType.DMA((2,))]
    return call(finish_kernel, "finish", out, scratch, held=False)(own, *received)


def per_device(
    query_in, key_in, value_in, short_taps, modal_residue, mode_damping_speed, skip_gain, out_weight
):
    channels = query_in.shape[0]
    n_ctx, n_ch = lax.axis_size("ctx"), lax.axis_size("ch")
    sibling = [(i, i ^ 1) for i in range(n_ch)]
    message, gated, params, basis, modes, order = states(
        key_in,
        value_in,
        query_in,
        jnp.transpose(short_taps, (0, 2, 1)),
        mode_damping_speed.T,
        modal_residue.T,
        skip_gain[None, :],
    )
    def across(value, by):
        return lax.ppermute(value, "ctx", [(i, i ^ by) for i in range(n_ctx)])

    swapped = [across(message, k) for k in (3, 2, 1)]
    tables = make_tables(query_in.shape[1], basis, modes)
    message, before, border = merge_four(message, swapped, params, tables)
    later, _ = lax.optimization_barrier((out_weight, message))
    far = lax.ppermute(later, "ch", sibling)
    theirs = across(message, PAIR)
    weight = weight_blocks(out_weight, message)
    message, before, border = merge_pair(message, theirs, before, border, params, tables, weight)
    local, gate, carry, reach = local_scan(gated, query_in, params, tables, order, message)
    messages = [message] + [across(message, k * ROW) for k in (2, 3, 1)]

    own = gate_all(messages, before, border, local, gate, carry, reach, params, tables)
    other = lax.ppermute(own, "ch", sibling)

    def swap(value, k):
        return lax.ppermute(value, "ch", [(i, i ^ (2 * k)) for i in range(n_ch)])

    operands = (near_sums(own, weight), other, far)
    over3, over1 = project(*operands, "opposite", [[(2, 1)], [(2, 0)]], BF16)
    over3, over1 = swap(over3, 3), swap(over1, 1)
    direct3, direct1, mine3, mine1 = sides(*operands)
    direct3, direct1 = swap(direct3, 3), swap(direct1, 1)
    (kept,) = project(*operands, "kept", [[(0, 0), (0, 1)]], F32)
    joined1 = swap(relay(over3, mine1), 1)
    joined3 = swap(relay(over1, mine3), 3)
    return finish(kept, direct1, direct3, joined1, joined3, order)


def solution(mesh):
    placed = (
        P("ch", "ctx"),
        P("ch", "ctx"),
        P("ch", "ctx"),
        P(None, "ch", None),
        P("ch", None),
        P("ch", None),
        P("ch"),
        P("ch", None),
    )
    return jax.shard_map(
        per_device, mesh=mesh, in_specs=placed, out_specs=P("ch", "ctx"), check_vma=False
    )
```

```python
import jax
import jax.numpy as jnp
from jax import lax
from jax.experimental import pallas as pl
from jax.experimental.pallas import tpu as pltpu
from jax.sharding import PartitionSpec as P

SEGMENTS = 8
LANES = 128
ORDER = 16
ROW = 8
SCOPED = 16 * 2**20
F32 = jnp.float32
BF16 = jnp.bfloat16
NT = (((1,), (1,)), ((), ()))
TN = (((0,), (0,)), ((), ()))

FOUR, PAIR = 4, 7
DECAY, FADE, WEIGHT, GROWTH = 0, 1, 4, 5
ALL, ALL_SEAM, AHEAD, AHEAD_SEAM, OVER_PAIR, OVER_Y = 7, 10, 13, 16, 18, 23
TABLES = 29
SKIP, FIRST = 9, 10
EDGES = 16


def call(kernel, name, out, scratch=(), held=True, outside=(), unread=()):
    whole = pl.BlockSpec(memory_space=pltpu.VMEM)
    if not held:
        whole = pl.BlockSpec(memory_space=pl.ANY)
    place = (lambda o: pltpu.VMEM(o.shape, o.dtype)) if held else (lambda o: o)

    def run(*args):
        spaces = [
            pl.ANY if i in unread else pltpu.HBM if i in outside else pltpu.VMEM
            for i in range(len(args))
        ]
        return pl.pallas_call(
            kernel,
            in_specs=[pl.BlockSpec(memory_space=space) for space in spaces],
            out_specs=jax.tree.map(lambda _: whole, out),
            out_shape=jax.tree.map(place, out),
            scratch_shapes=list(scratch),
            compiler_params=pltpu.CompilerParams(vmem_limit_bytes=SCOPED),
            name=name,
        )(*(pltpu.with_memory_space_constraint(a, space) for a, space in zip(args, spaces)))

    return run


def order_matrix(span):
    steps = span // SEGMENTS
    row = lax.broadcasted_iota(jnp.int32, (span, span), 0)
    col = lax.broadcasted_iota(jnp.int32, (span, span), 1)
    return jnp.where(col == (row & (SEGMENTS - 1)) * steps + (row >> 3), 1.0, 0.0).astype(BF16)


def segment_index():
    return lax.broadcasted_iota(jnp.int32, (SEGMENTS, LANES), 0)


def by_group(channels, body):
    def step(g, nothing):
        body(pl.ds(pl.multiple_of(g * LANES, LANES), LANES))
        return nothing

    lax.fori_loop(0, channels // LANES, step, 0)


def place_of():
    here = lax.axis_index("ctx")
    return here // ROW, lax.rem(here, ROW)


def tables_kernel(span, basis, modes, tables):
    y, z = place_of()
    damping, residue = modes[0], modes[1]

    def fade(by):
        return jnp.exp(-damping * by)

    def only(flag, value):
        return jnp.where(flag, value, 0.0)

    for i in range(4):
        tables[DECAY + i] = basis[i]
    tables[WEIGHT] = residue * jnp.sqrt(damping)
    tables[GROWTH] = fade(-1.0)
    tables[GROWTH + 1] = fade(-2.0)
    place = z & (FOUR - 1)
    for q in range(3):
        tables[ALL + q] = fade(float((3 - q) * span))
        tables[ALL_SEAM + q] = fade(float((3 - q) * span - 2))
        ahead = jnp.maximum(place - 1 - q, 0) * span
        tables[AHEAD + q] = only(q < place, fade(ahead.astype(F32)))
    for q in range(2):
        seen = jnp.maximum((place - 1 - q) * span - 2, 0)
        tables[AHEAD_SEAM + q] = only(q + 1 < place, fade(seen.astype(F32)))
    older = (z & FOUR) != 0
    ahead = place * span
    whole = fade(float(FOUR * span))
    tables[OVER_PAIR] = only(older, fade(ahead.astype(F32)))
    seen = jnp.maximum(ahead - 2, 0).astype(F32)
    tables[OVER_PAIR + 1] = only(older & (ahead > 0), fade(seen))
    tables[OVER_PAIR + 2] = jnp.where(older, whole, 1.0)
    tables[OVER_PAIR + 3] = jnp.where(older, 1.0, whole)
    tables[OVER_PAIR + 4] = fade(float(FOUR * span - 2))
    for s in range(3):
        ahead = (ROW * s + z) * span
        tables[OVER_Y + s] = only(y >= s + 1, fade(ahead.astype(F32)))
        seen = jnp.maximum(ahead - 2, 0).astype(F32)
        tables[OVER_Y + 3 + s] = only((y >= s + 1) & (ahead > 0), fade(seen))


def make_tables(span, basis, modes):
    out = jax.ShapeDtypeStruct((TABLES, *basis.shape[1:]), F32)
    return call(lambda *refs: tables_kernel(span, *refs), "tables", out)(basis, modes)


def states_kernel(
    key_hbm,
    value_hbm,
    query_hbm,
    taps_hbm,
    damping_hbm,
    residue_hbm,
    skip_hbm,
    message,
    gated,
    params,
    basis,
    modes,
    order,
    raw,
    tail,
    taps_in,
    skip,
    streams,
    state,
    edges,
    start_fade,
    sems,
):
    channels, span = key_hbm.shape
    steps = span // SEGMENTS
    fixed = [
        pltpu.make_async_copy(src, dst, sems.at[i])
        for i, (src, dst) in enumerate(
            (
                (damping_hbm, modes.at[0]),
                (taps_hbm, taps_in),
                (residue_hbm, modes.at[1]),
                (skip_hbm, skip),
                (query_hbm.at[:, span - LANES :], tail),
            )
        )
    ]

    big = [
        pltpu.make_async_copy(src, raw.at[s], sems.at[len(fixed) + s])
        for s, src in enumerate((key_hbm, value_hbm))
    ]
    for c in fixed[:2]:
        c.start()
    for c in big:
        c.start()
    for c in fixed[2:]:
        c.start()
    order[...] = order_matrix(span)
    segment = segment_index()
    params[...] = jnp.zeros_like(params)
    edges[...] = jnp.zeros_like(edges)
    for c in big + fixed:
        c.wait()
    for s in range(2):
        streams[s] = lax.dot_general(order[...], raw[s], NT, preferred_element_type=F32)
    basis[DECAY] = jnp.exp(-modes[0])
    for i in range(3):
        basis[FADE + i] = jnp.exp(-modes[0] * float(steps << i))
    start_fade[...] = jnp.exp(-modes[0] * float(span - 2))
    for i in range(9):
        params[i : i + 1, :] = taps_in[(1 + i // 3) % 3, i % 3, :][None, :]
    params[SKIP : SKIP + 1, :] = skip[...]
    for s in range(2):
        edges[2 * s : 2 * s + 1, :] = streams[s, 0:1, :]
        edges[2 * s + 1 : 2 * s + 2, :] = streams[s, SEGMENTS : SEGMENTS + 1, :]
        edges[4 + 2 * s : 5 + 2 * s, :] = streams[s, span - SEGMENTS - 1 : span - SEGMENTS, :]
        edges[5 + 2 * s : 6 + 2 * s, :] = streams[s, span - 1 : span, :]
    row = lax.broadcasted_iota(jnp.int32, (8, LANES), 0)
    col = lax.broadcasted_iota(jnp.int32, (8, LANES), 1)
    pick = jnp.where(col == LANES - 2 + row, 1.0, 0.0).astype(BF16)
    edges[8:16, :] = lax.dot_general(pick, tail[...], NT, preferred_element_type=F32)
    message[EDGES:, :] = edges[...].astype(BF16)

    def group(lanes):
        taps = [params[i : i + 1, lanes] for i in range(6)]
        decay = [basis[DECAY, r : r + 1, lanes] for r in range(ORDER)]

        def at(s, a):
            if a >= 0:
                return streams[s, a * SEGMENTS : (a + 1) * SEGMENTS, lanes]
            rolled = pltpu.roll(at(s, a + steps), 1, 0)
            return jnp.where(segment == 0, 0.0, rolled)

        held = [jnp.zeros((SEGMENTS, LANES), F32) for _ in range(ORDER)]
        for a in range(steps):
            f = [
                taps[3 * s] * at(s, a)
                + taps[3 * s + 1] * at(s, a - 1)
                + taps[3 * s + 2] * at(s, a - 2)
                for s in range(2)
            ]
            u = f[0] * f[1]
            if a < 2:
                params[FIRST + a : FIRST + a + 1, lanes] = f[0][0:1]
                params[FIRST + 2 + a : FIRST + 3 + a, lanes] = f[1][0:1]
                u = jnp.where(segment == 0, 0.0, u)
            gated[a * SEGMENTS : (a + 1) * SEGMENTS, lanes] = u
            for r in range(ORDER):
                held[r] = held[r] * decay[r] + u
        for r in range(ORDER):
            total = held[r]
            for i in range(3):
                fade = basis[FADE + i, r : r + 1, lanes]
                total = total + fade * pltpu.roll(total, 1 << i, 0)
            state[r : r + 1, lanes] = total[SEGMENTS - 1 :]

    by_group(channels, group)
    at = lambda i: params[FIRST + i : FIRST + i + 1, :]
    start = start_fade[...] * (basis[DECAY] * (at(0) * at(2)) + at(1) * at(3))
    total = state[...] + jnp.where(lax.axis_index("ctx") == 0, start, 0.0)
    message[0:ORDER, :] = total.astype(BF16)


def states(key_in, value_in, query_in, taps, damping, residue, skip):
    channels, span = key_in.shape
    shape = jax.ShapeDtypeStruct
    out = [
        shape((EDGES + 16, channels), BF16),
        shape((span, channels), F32),
        shape((16, channels), F32),
        shape((4, ORDER, channels), F32),
        shape((2, ORDER, channels), F32),
        shape((span, span), BF16),
    ]
    scratch = [
        pltpu.VMEM((2, channels, span), BF16),
        pltpu.VMEM((channels, LANES), BF16),
        pltpu.VMEM(taps.shape, F32),
        pltpu.VMEM(skip.shape, F32),
        pltpu.VMEM((2, span, channels), F32),
        pltpu.VMEM((ORDER, channels), F32),
        pltpu.VMEM((16, channels), F32),
        pltpu.VMEM((ORDER, channels), F32),
        pltpu.SemaphoreType.DMA((7,)),
    ]
    return call(states_kernel, "states", out, scratch, outside=range(7))(
        key_in, value_in, query_in, taps, damping, residue, skip
    )


def local_kernel(
    gated,
    query_hbm,
    params,
    tables,
    order,
    after,
    local,
    gate,
    carry,
    reach,
    raw,
    stream,
    sem,
):
    channels, span = query_hbm.shape
    steps = span // SEGMENTS
    copy = pltpu.make_async_copy(query_hbm, raw, sem)
    copy.start()
    copy.wait()
    stream[...] = lax.dot_general(order[...], raw[...], NT, preferred_element_type=F32)
    segment = segment_index()

    def group(lanes):
        taps = [params[6 + i : 7 + i, lanes] for i in range(3)]
        skip = params[SKIP : SKIP + 1, lanes]
        decay = [tables[DECAY, r : r + 1, lanes] for r in range(ORDER)]
        weight = [tables[WEIGHT, r : r + 1, lanes] for r in range(ORDER)]

        def at(a):
            if a >= 0:
                return stream[a * SEGMENTS : (a + 1) * SEGMENTS, lanes]
            rolled = pltpu.roll(at(a + steps), 1, 0)
            return jnp.where(segment == 0, 0.0, rolled)

        held = [jnp.zeros((SEGMENTS, LANES), F32) for _ in range(ORDER)]
        for a in range(steps):
            here = slice(a * SEGMENTS, (a + 1) * SEGMENTS)
            u = gated[here, lanes]
            parts = [skip * u, None, None, None]
            for r in range(ORDER):
                held[r] = held[r] * decay[r] + u
                term = weight[r] * held[r]
                parts[r % 4] = term if parts[r % 4] is None else parts[r % 4] + term
            local[here, lanes] = (parts[0] + parts[1]) + (parts[2] + parts[3])
            gate[here, lanes] = taps[0] * at(a) + taps[1] * at(a - 1) + taps[2] * at(a - 2)
        for r in range(ORDER):
            total = held[r]
            far = jnp.ones((SEGMENTS, LANES), F32)
            for i in range(3):
                fade = tables[FADE + i, r : r + 1, lanes]
                by = 1 << i
                total = total + jnp.where(segment < by, 0.0, fade * pltpu.roll(total, by, 0))
                far = jnp.where((segment & by) != 0, far * fade, far)
            total = jnp.where(segment < 1, 0.0, pltpu.roll(total, 1, 0))
            here = slice(r * SEGMENTS, (r + 1) * SEGMENTS)
            scale = weight[r] * decay[r]
            carry[here, lanes] = scale * total
            reach[here, lanes] = scale * far

    by_group(channels, group)


def local_scan(gated, query_in, params, tables, order, after):
    channels, span = query_in.shape
    shape = jax.ShapeDtypeStruct
    out = [
        shape((span, channels), F32),
        shape((span, channels), F32),
        shape((ORDER * SEGMENTS, channels), F32),
        shape((ORDER * SEGMENTS, channels), F32),
    ]
    scratch = [
        pltpu.VMEM((channels, span), BF16),
        pltpu.VMEM((span, channels), F32),
        pltpu.SemaphoreType.DMA,
    ]
    return call(local_kernel, "local_scan", out, scratch, outside=(1,), unread=(5,))(
        gated, query_in, params, tables, order, after
    )


def unpack(message):
    return message[0:ORDER, :].astype(F32), message[EDGES:, :].astype(F32)


def gated_start(params, new, old):
    out = []
    for s in range(2):
        near, mid, far = (params[3 * s + i : 3 * s + i + 1, :] for i in range(3))
        first, second = new[2 * s : 2 * s + 1], new[2 * s + 1 : 2 * s + 2]
        before, last = old[4 + 2 * s : 5 + 2 * s], old[5 + 2 * s : 6 + 2 * s]
        out.append(
            (near * first + mid * last + far * before, near * second + mid * first + far * last)
        )
    (k0, k1), (v0, v1) = out
    return k0 * v0, k1 * v1


def in_order(place, mine, swapped):
    one, two, three = swapped
    pick = lambda q, m, a, b, c: jnp.where(
        place == q, m, jnp.where((place ^ 1) == q, a, jnp.where((place ^ 2) == q, b, c))
    )
    return [
        tuple(pick(q, m, a, b, c) for m, a, b, c in zip(mine, one, two, three)) for q in range(4)
    ]


def send(message, state, first, last):
    message[0:ORDER, :] = state.astype(BF16)
    row = lax.broadcasted_iota(jnp.int32, first.shape, 0)
    message[EDGES:, :] = jnp.where(row < 4, first, last).astype(BF16)


def merge_four_kernel(mine, three, two, one, params, tables, message, before, border):
    _, z = place_of()
    place = z & (FOUR - 1)
    blocks = in_order(place, unpack(mine), [unpack(m) for m in (one, two, three)])
    total, ahead = blocks[3][0], jnp.zeros_like(before)
    for q in range(3):
        total = total + tables[ALL + q] * blocks[q][0]
        ahead = ahead + tables[AHEAD + q] * blocks[q][0]
        u0, u1 = gated_start(params, blocks[q + 1][1], blocks[q][1])
        seam = tables[DECAY] * u0 + u1
        total = total + tables[ALL_SEAM + q] * seam
        if q < 2:
            ahead = ahead + tables[AHEAD_SEAM + q] * seam
    send(message, total, blocks[0][1], blocks[3][1])
    before[...] = ahead
    last = jnp.zeros_like(border)
    for q in range(3):
        last = jnp.where(place == q + 1, blocks[q][1], last)
    border[...] = last


def merge_four(mine, swapped, params, tables):
    channels = mine.shape[1]
    shape = jax.ShapeDtypeStruct
    out = [shape(mine.shape, BF16), shape((ORDER, channels), F32), shape((16, channels), F32)]
    return call(merge_four_kernel, "merge_four", out)(mine, *swapped, params, tables)


def merge_pair_kernel(
    mine, theirs, before, border, params, tables, after, message, before_out, border_out
):
    at = OVER_PAIR
    _, z = place_of()
    older = (z & FOUR) != 0
    first = (z & (FOUR - 1)) == 0
    my_state, my_edges = unpack(mine)
    state, edges = unpack(theirs)
    new = jnp.where(older, my_edges, edges)
    old = jnp.where(older, edges, my_edges)
    u0, u1 = gated_start(params, new, old)
    seam = tables[DECAY] * u0 + u1
    total = tables[at + 2] * state + tables[at + 3] * my_state + tables[at + 4] * seam
    send(message, total, old, new)
    before_out[...] = before[...] + tables[at] * state + tables[at + 1] * seam
    border_out[...] = jnp.where(older & first, edges, border[...])


def merge_pair(mine, theirs, before, border, params, tables, after):
    shape = jax.ShapeDtypeStruct
    out = [shape(mine.shape, BF16), shape(before.shape, F32), shape(border.shape, F32)]
    return call(merge_pair_kernel, "merge_pair", out, unread=(6,))(
        mine, theirs, before, border, params, tables, after
    )


def gate_kernel(
    mine,
    row2,
    row3,
    row1,
    before_in,
    border_in,
    local,
    gate,
    carry,
    reach,
    params,
    tables,
    out,
    before,
    starts,
):
    span, channels = local.shape
    steps = span // SEGMENTS
    y, z = place_of()
    lying = in_order(y, unpack(mine), [unpack(m) for m in (row1, row2, row3)])
    rows = [unpack(mine)]
    for s in range(1, 4):
        pick = lambda a, b, c: jnp.where(y - s == 0, a, jnp.where(y - s == 1, b, c))
        rows.append(tuple(pick(a, b, c) for a, b, c in zip(*lying[:3])))
    total = before_in[...]
    for s in range(3):
        u0, u1 = gated_start(params, rows[s][1], rows[s + 1][1])
        total = total + tables[OVER_Y + s] * rows[s + 1][0]
        total = total + tables[OVER_Y + 3 + s] * (tables[DECAY] * u0 + u1)
    border = jnp.where((z == 0) & (y >= 1), rows[1][1], border_in[...])
    u = [None, None]
    p = lambda i: params[i : i + 1, :]
    e = lambda i: border[4 + i : 5 + i]
    u[0] = (p(FIRST) + p(1) * e(1) + p(2) * e(0)) * (p(FIRST + 2) + p(4) * e(3) + p(5) * e(2))
    u[1] = (p(FIRST + 1) + p(2) * e(1)) * (p(FIRST + 3) + p(5) * e(3))
    before[...] = total + tables[GROWTH] * u[0] + tables[GROWTH + 1] * u[1]
    grown = jnp.sum(tables[WEIGHT] * tables[GROWTH], axis=0, keepdims=True)
    starts[0:1, :] = p(SKIP) * u[0] - grown * u[1]
    starts[1:2, :] = p(SKIP) * u[1]
    starts[2:3, :] = p(7) * e(5) + p(8) * e(4)
    starts[3:4, :] = p(8) * e(5)
    segment = segment_index()

    def group(lanes):
        decay, term = [], []
        for r in range(ORDER):
            here = slice(r * SEGMENTS, (r + 1) * SEGMENTS)
            term.append(carry[here, lanes] + reach[here, lanes] * before[r : r + 1, lanes])
            decay.append(tables[DECAY, r : r + 1, lanes])
        for pair in range(steps // 2):
            both = []
            for a in (2 * pair, 2 * pair + 1):
                here = slice(a * SEGMENTS, (a + 1) * SEGMENTS)
                parts = [local[here, lanes], None, None, None]
                times = gate[here, lanes]
                if a < 2:
                    first = segment == 0
                    parts[0] = parts[0] + jnp.where(first, starts[a : a + 1, lanes], 0.0)
                    times = times + jnp.where(first, starts[2 + a : 3 + a, lanes], 0.0)
                for r in range(ORDER):
                    parts[r % 4] = term[r] if parts[r % 4] is None else parts[r % 4] + term[r]
                    term[r] = term[r] * decay[r]
                both.append(((parts[0] + parts[1]) + (parts[2] + parts[3])) * times)
            here = slice(pair * 2 * SEGMENTS, (pair + 1) * 2 * SEGMENTS)
            out[here, lanes] = jnp.concatenate(both, axis=0).astype(BF16)

    by_group(channels, group)


def gate_all(messages, before, border, local, gate, carry, reach, params, tables):
    out = jax.ShapeDtypeStruct(local.shape, BF16)
    scratch = [pltpu.VMEM(before.shape, F32), pltpu.VMEM((8, before.shape[1]), F32)]
    return call(gate_kernel, "gated", out, scratch)(
        *messages, before, border, local, gate, carry, reach, params, tables
    )


def blocks_kernel(weight_hbm, after, out, sems):
    columns = out.shape[1] // sems.shape[0]
    me = lax.axis_index("ch")
    copies = []
    for k in range(sems.shape[0]):
        at = pl.ds(pl.multiple_of((me ^ (2 * k)) * columns, columns), columns)
        copies.append(
            pltpu.make_async_copy(
                weight_hbm.at[:, at], out.at[:, k * columns : (k + 1) * columns], sems.at[k]
            )
        )
    for c in copies:
        c.start()
    for c in copies:
        c.wait()


def weight_blocks(weight, after):
    channels, width = weight.shape
    chips = lax.axis_size("ch") // 2
    out = jax.ShapeDtypeStruct((channels, width // 2), BF16)
    scratch = [pltpu.SemaphoreType.DMA((chips,))]
    return call(blocks_kernel, "weight_blocks", out, scratch, outside=(0,), unread=(1,))(weight, after)


def near_kernel(mine, weight, out):
    out[...] = jnp.dot(mine[...], weight[...], preferred_element_type=F32)


def near_sums(mine, weight):
    out = jax.ShapeDtypeStruct((mine.shape[0], weight.shape[1]), F32)
    return call(near_kernel, "near_sums", out)(mine, weight)


def project(near, other, far, name, wanted, dtype):
    span = near.shape[0]
    half = span // 2
    columns = far.shape[1] // lax.axis_size("ch")

    def kernel(near_ref, other_ref, far_ref, *out_refs):
        for out_ref, parts in zip(out_refs, wanted):
            for i, (k, part) in enumerate(parts):
                block = lax.axis_index("ch") ^ (2 * k)
                there = pl.ds(pl.multiple_of(block * columns, columns), columns)
                rows = slice(part * half, (part + 1) * half)
                total = near_ref[rows, k * columns : (k + 1) * columns] + jnp.dot(
                    other_ref[rows, :], far_ref[:, there], preferred_element_type=F32
                )
                out_ref[i * half : (i + 1) * half, :] = total.astype(dtype)

    out = [jax.ShapeDtypeStruct((half * len(parts), columns), dtype) for parts in wanted]
    return call(kernel, name, out)(near, other, far)


def sides(near, other, far):
    span = near.shape[0]
    half = span // 2
    columns = far.shape[1] // lax.axis_size("ch")

    def kernel(near_ref, other_ref, far_ref, direct3, direct1, mine3, mine1):
        for k, direct, mine in ((3, direct3, mine3), (1, direct1, mine1)):
            block = lax.axis_index("ch") ^ (2 * k)
            there = pl.ds(pl.multiple_of(block * columns, columns), columns)
            total = near_ref[:, k * columns : (k + 1) * columns] + jnp.dot(
                other_ref[...], far_ref[:, there], preferred_element_type=F32
            )
            top, low = total[:half], total[half:]
            direct[...] = (low if k == 3 else top).astype(BF16)
            mine[...] = top if k == 3 else low

    out = [jax.ShapeDtypeStruct((half, columns), d) for d in (BF16, BF16, F32, F32)]
    return call(kernel, "sides", out)(near, other, far)


def opposite(near, other, far):
    half = near.shape[0] // 2
    columns = far.shape[1] // lax.axis_size("ch")

    def kernel(near_ref, other_ref, far_ref, over3, over1):
        block = lax.axis_index("ch") ^ 4
        there = pl.ds(pl.multiple_of(block * columns, columns), columns)
        total = near_ref[:, 2 * columns : 3 * columns] + jnp.dot(
            other_ref[...], far_ref[:, there], preferred_element_type=F32
        )
        over1[...] = total[:half].astype(BF16)
        over3[...] = total[half:].astype(BF16)

    out = [jax.ShapeDtypeStruct((half, columns), BF16)] * 2
    return call(kernel, "opposite", out)(near, other, far)


def relay_kernel(passing, own, out):
    out[...] = (passing[...].astype(F32) + own[...]).astype(BF16)


def relay(passing, own):
    return call(relay_kernel, "relay", jax.ShapeDtypeStruct(own.shape, BF16))(passing, own)


def finish_kernel(own, direct1, direct3, joined1, joined3, order, out, result, sems):
    half = joined1.shape[0]
    columns = own.shape[1]
    copies = []
    for i in range(2):
        here = slice(i * columns // 2, (i + 1) * columns // 2)
        top = own[0:half, here] + (direct1[:, here].astype(F32) + joined3[:, here].astype(F32))
        low = own[half:, here] + (direct3[:, here].astype(F32) + joined1[:, here].astype(F32))
        total = jnp.concatenate([top.astype(BF16), low.astype(BF16)], axis=0)
        result[here, :] = lax.dot_general(
            total, order[...], TN, preferred_element_type=F32
        ).astype(BF16)
        copies.append(pltpu.make_async_copy(result.at[here, :], out.at[here, :], sems.at[i]))
        copies[-1].start()
    for c in copies:
        c.wait()


def finish(own, *received):
    span, columns = own.shape
    out = jax.ShapeDtypeStruct((columns, span), BF16)
    scratch = [pltpu.VMEM(out.shape, BF16), pltpu.SemaphoreType.DMA((2,))]
    return call(finish_kernel, "finish", out, scratch, held=False)(own, *received)


def per_device(
    query_in, key_in, value_in, short_taps, modal_residue, mode_damping_speed, skip_gain, out_weight
):
    channels = query_in.shape[0]
    n_ctx, n_ch = lax.axis_size("ctx"), lax.axis_size("ch")
    sibling = [(i, i ^ 1) for i in range(n_ch)]
    message, gated, params, basis, modes, order = states(
        key_in,
        value_in,
        query_in,
        jnp.transpose(short_taps, (0, 2, 1)),
        mode_damping_speed.T,
        modal_residue.T,
        skip_gain[None, :],
    )
    def across(value, by):
        return lax.ppermute(value, "ctx", [(i, i ^ by) for i in range(n_ctx)])

    swapped = [across(message, k) for k in (3, 2, 1)]
    tables = make_tables(query_in.shape[1], basis, modes)
    message, before, border = merge_four(message, swapped, params, tables)
    later, _ = lax.optimization_barrier((out_weight, message))
    far = lax.ppermute(later, "ch", sibling)
    theirs = across(message, PAIR)
    weight = weight_blocks(out_weight, message)
    message, before, border = merge_pair(message, theirs, before, border, params, tables, weight)
    local, gate, carry, reach = local_scan(gated, query_in, params, tables, order, message)
    messages = [message] + [across(message, k * ROW) for k in (2, 3, 1)]

    own = gate_all(messages, before, border, local, gate, carry, reach, params, tables)
    other = lax.ppermute(own, "ch", sibling)

    def swap(value, k):
        return lax.ppermute(value, "ch", [(i, i ^ (2 * k)) for i in range(n_ch)])

    operands = (near_sums(own, weight), other, far)
    over3, over1 = opposite(*operands)
    over3, over1 = swap(over3, 3), swap(over1, 1)
    direct3, direct1, mine3, mine1 = sides(*operands)
    direct3, direct1 = swap(direct3, 3), swap(direct1, 1)
    (kept,) = project(*operands, "kept", [[(0, 0), (0, 1)]], F32)
    joined1 = swap(relay(over3, mine1), 1)
    joined3 = swap(relay(over1, mine3), 3)
    return finish(kept, direct1, direct3, joined1, joined3, order)


def solution(mesh):
    placed = (
        P("ch", "ctx"),
        P("ch", "ctx"),
        P("ch", "ctx"),
        P(None, "ch", None),
        P("ch", None),
        P("ch", None),
        P("ch"),
        P("ch", None),
    )
    return jax.shard_map(
        per_device, mesh=mesh, in_specs=placed, out_specs=P("ch", "ctx"), check_vma=False
    )
```
